32 devices in a mesh: group: 4 (over y, x), dom: 8 (over z, core).
Axes of the slice: x: 2, y: 2, z: 4, core: 2. Of those that a mesh axis runs over, the one named last changes fastest.
Arguments:
- mode_shapes: float32 [96, 65536], P(None, ('group', 'dom')), may hold values from -6 to 6
- send_nodes: int32 [32, 1024], P(('group', 'dom')), may hold values from 0 to 2047, as said below
- interp_index: int32 [8, 64, 4096], P(None, 'group', 'dom'), may hold values from -1 to 1023, as said below
- interp_weight: float32 [8, 64, 4096], P(None, 'group', 'dom'), may hold values from 0.1 to 1
- blend: float32 [64, 4096], P('group', 'dom'), may hold values from 0.2 to 1
- motion_gain: float32 [30, 64, 4096], P(None, 'group', 'dom'), may hold values from -3 to 3
- frequency: float32 [32], replicated, may hold values from 0.3 to 3
- volume: float32 [64, 4096], P('group', 'dom'), may hold values from 0.5 to 2
- jacobian: float32 [125, 64, 4096], P(None, 'group', 'dom'), may hold values from -1.2 to 1.2
- state: bfloat16 [320, 64, 4096], P(None, 'group', 'dom'), may hold values from -6 to 6
Outputs:
- mesh_motion: float32 [96, 64, 4096], P(None, 'group', 'dom')
- residual: float32 [320, 64, 4096], P(None, 'group', 'dom')
The draws below stay inside these ranges and needn't reach their ends.
Inputs may be any that keep to these rules, and one draw needn't show every extreme that they name: `send_nodes`: each entry names a node local to the owner of its row, 0 to 2047. `interp_index`: A live entry is s * 32 + t, naming slot t that owner s sends to the cell's partition; a cell has 1 to 8 live entries, stored first, then -1 for padding; some cell has all 8 live. From each owner a partition uses at most 32 slots.
All inputs are finite; a program needn't handle non-finite values.
Results may differ from the reference program's by a relative error of at most 0.0003.
Values may be sent and summed in bfloat16 or wider, within the bound.
No kernel may reach another device: no remote copies, remote signals or barrier semaphores. Data moves between devices by JAX's collectives and lax.ppermute only.
A program may use at most 192 MiB of HBM per device.

```python
import math
import jax
import jax.numpy as jnp

COMP = 3
VARS = 5
KST = 8
SLOT = 32
NS_DEV = 2048
BI = 16
BJ = 512
CASES = 32
NS = 65536
NI = 64
NJ = 4096
N_DOM = 8
DEVICES = 32


def coupling_tables(key):
    keys = jax.random.split(jax.random.fold_in(key, 7), 9)
    load = jax.random.randint(keys[0], (DEVICES,), 2, 6)
    base = jax.random.randint(keys[1], (DEVICES, DEVICES), 0, SLOT // 2 + 1)
    counts = jnp.clip(base * load[None, :] // 2, 1, SLOT)
    first_src = jax.random.randint(keys[2], (), 0, DEVICES)
    first_dst = jax.random.randint(keys[3], (), 0, DEVICES)
    full_dst = jax.random.randint(keys[4], (), 0, DEVICES)
    source = jnp.arange(DEVICES)[:, None]
    target = jnp.arange(DEVICES)[None, :]
    counts = jnp.where((source == first_src) & (target == first_dst) | (target == full_dst), SLOT, counts)
    counts = jnp.where((source == DEVICES - 1) & (target == 0), SLOT, counts)
    nodes = jax.random.randint(keys[5], (DEVICES, DEVICES * SLOT), 0, NS_DEV).astype(jnp.int32)
    nlive = jax.random.randint(keys[6], (NI, NJ), 1, KST + 1)
    nlive = nlive.at[0, 0].set(KST)
    owners = jax.random.randint(keys[7], (KST, NI, NJ), 0, DEVICES)
    cell_part = (jnp.arange(NI) // BI)[:, None] * N_DOM + (jnp.arange(NJ) // BJ)[None, :]
    avail = counts[owners, jnp.broadcast_to(cell_part[None], (KST, NI, NJ))]
    pick = jax.random.randint(keys[8], (KST, NI, NJ), 0, 1 << 20) % avail
    flat = owners * SLOT + pick
    order = jnp.arange(KST)[:, None, None]
    index = jnp.where(order < nlive[None], flat, -1).astype(jnp.int32)
    full_index = index.at[0, 0, 0].set(DEVICES * SLOT - 1)
    return (nodes, full_index)


def draw_send_nodes(key, part):
    return coupling_tables(key)[0]


def draw_interp_index(key, part):
    return coupling_tables(key)[1]


def steps_of(stream_key, extent, shards, smallest, top_value):
    def one(position, shards_of):
        draws = jax.random.uniform(jax.random.fold_in(jax.random.fold_in(stream_key, 6), position), (shards_of,), jnp.float32, smallest / len(shards), top_value / len(shards))
        return jnp.repeat(jnp.exp(draws), extent[position] // shards_of).reshape((-1,) + (1,) * (len(extent) - position - 1))

    loudness = one(*shards[0])
    for cut in shards[1:]:
        loudness = loudness * one(*cut)
    return loudness


def bell_draw(rng, shape, width, most, cuts=(), kind=jnp.bfloat16):
    entries = width * jax.random.normal(rng, shape, jnp.float32)
    if cuts:
        entries = entries * steps_of(rng, shape, cuts, -0.22, 0.18)
    return jnp.clip(entries, -most, most).astype(kind)


def setup_inputs(seed: int = 0) -> dict:
    arg_keys = jax.random.split(jax.random.key(seed), 11)
    return {
        "mode_shapes": bell_draw(arg_keys[0], (CASES * COMP, NS), 1.0, 6.0, ((1, 32),), jnp.float32),
        "send_nodes": draw_send_nodes(jax.random.fold_in(arg_keys[10], 71), 0),
        "interp_index": draw_interp_index(jax.random.fold_in(arg_keys[10], 71), 0),
        "interp_weight": jnp.clip(0.1 + 0.9 * jax.random.uniform(arg_keys[3], (KST, NI, NJ), jnp.float32) ** steps_of(arg_keys[3], (KST, NI, NJ), ((1, 4), (2, 8)), -0.2, 0.2), 0.1, 1.0),
        "blend": jnp.clip(0.2 + 0.8 * jax.random.uniform(arg_keys[4], (NI, NJ), jnp.float32) ** steps_of(arg_keys[4], (NI, NJ), ((0, 4), (1, 8)), -0.2, 0.2), 0.2, 1.0),
        "motion_gain": bell_draw(arg_keys[5], (2 * VARS * COMP, NI, NJ), 0.5, 3.0, ((1, 4), (2, 8)), jnp.float32),
        "frequency": jnp.clip(jnp.exp(jax.random.uniform(arg_keys[6], (CASES,), jnp.float32, math.log(0.3), math.log(3.0))), 0.3, 3.0),
        "volume": jnp.clip(jnp.exp(math.log(2.0) - 1.3862944 * jax.random.uniform(arg_keys[7], (NI, NJ), jnp.float32) ** steps_of(arg_keys[7], (NI, NJ), ((0, 4), (1, 8)), -0.2, 0.2)), 0.5, 2.0),
        "jacobian": bell_draw(arg_keys[8], (5 * VARS * VARS, NI, NJ), 0.2, 1.2, ((1, 4), (2, 8)), jnp.float32),
        "state": bell_draw(arg_keys[9], (CASES * 2 * VARS, NI, NJ), 1.0, 6.0, ((1, 4), (2, 8))),
    }


def apply_block(block, field):
    total = jnp.zeros(field.shape, jnp.float32)
    for u in range(VARS):
        total = total + block[:, u][None, None] * field[:, :, u][:, :, None]
    return total


def reference(mode_shapes, send_nodes, interp_index, interp_weight, blend, motion_gain, frequency, volume, jacobian, state):
    rows = jnp.arange(NI, dtype=jnp.int32) // BI
    cols = jnp.arange(NJ, dtype=jnp.int32) // BJ
    partition = rows[:, None] * N_DOM + cols[None, :]
    live = interp_index >= 0
    safe = jnp.maximum(interp_index, 0)
    weight = jnp.where(live, interp_weight, jnp.float32(0.0))
    scaled = weight * (blend / jnp.sum(weight, axis=0))[None]
    motion = jnp.zeros((CASES * COMP, NI, NJ), jnp.float32)
    for k in range(KST):
        owner = safe[k] // SLOT
        slot = safe[k] % SLOT
        node = send_nodes[owner, partition * SLOT + slot] + owner * NS_DEV
        motion = motion + scaled[k][None] * mode_shapes[:, node]
    gain = motion_gain.reshape(2, VARS, COMP, NI, NJ)
    disp = motion.reshape(CASES, COMP, NI, NJ)
    pos_force = jnp.zeros((CASES, VARS, NI, NJ), jnp.float32)
    vel_force = jnp.zeros((CASES, VARS, NI, NJ), jnp.float32)
    for x in range(COMP):
        pos_force = pos_force + gain[0, :, x][None] * disp[:, x][:, None]
        vel_force = vel_force + gain[1, :, x][None] * disp[:, x][:, None]
    field = state.astype(jnp.float32).reshape(CASES, 2, VARS, NI, NJ)
    blocks = jacobian.reshape(5, VARS, VARS, NI, NJ)
    padded = jnp.pad(field, ((0, 0), (0, 0), (0, 0), (1, 1), (1, 1)))
    flux = apply_block(blocks[0], field)
    flux = flux + apply_block(blocks[1], padded[:, :, :, :-2, 1:-1])
    flux = flux + apply_block(blocks[2], padded[:, :, :, 2:, 1:-1])
    flux = flux + apply_block(blocks[3], padded[:, :, :, 1:-1, :-2])
    flux = flux + apply_block(blocks[4], padded[:, :, :, 1:-1, 2:])
    omega = frequency[:, None, None, None]
    real_part = flux[:, 0] - omega * volume[None, None] * field[:, 1] + pos_force
    imag_part = flux[:, 1] + omega * volume[None, None] * field[:, 0] + omega * vel_force
    residual = jnp.stack([real_part, imag_part], axis=1).reshape(CASES * 2 * VARS, NI, NJ)
    return motion, residual
```

```python
import functools
import jax
import jax.numpy as jnp
from jax import lax
from jax.experimental import pallas as pl
from jax.experimental.pallas import tpu as pltpu
from jax.sharding import PartitionSpec as P

COMP = 3
VARS = 5
PARTS = 2
LANES = 128
SUB = 8
F32 = jnp.float32
BF16 = jnp.bfloat16


def halves(value):
    hi = value.astype(BF16)
    lo = (value - hi.astype(F32)).astype(BF16)
    return hi, lo


def diagonal(rows, cols, offset):
    r = lax.broadcasted_iota(jnp.int32, (rows, cols), 0)
    c = lax.broadcasted_iota(jnp.int32, (rows, cols), 1)
    return jnp.where(r + offset == c, 1.0, 0.0).astype(BF16)


def outgoing_kernel(modes, nodes, state, table, top, bottom, first, last, split, picked):
    width, owned = modes.shape
    planes, rows, cols = state.shape
    listed = nodes.shape[1]

    @pl.when(pl.program_id(0) == 0)
    def _():
        hi, lo = halves(modes[...])
        split[0:width] = hi
        split[width:] = lo
        step = min(listed, 256)
        node_rows = lax.broadcasted_iota(jnp.int32, (owned, step), 0)

        def pick(b, _):
            at = pl.ds(pl.multiple_of(b * step, step), step)
            onehot = jnp.where(node_rows == nodes[:, at], 1.0, 0.0).astype(BF16)
            picked[...] = jnp.dot(split[...], onehot, preferred_element_type=F32)
            table[at, :] = picked[...].T.astype(BF16)
            return 0

        lax.fori_loop(0, listed // step, pick, 0)

    r = lax.broadcasted_iota(jnp.int32, (32, 16 * rows), 0)
    c = lax.broadcasted_iota(jnp.int32, (32, 16 * rows), 1)
    want = jnp.where(r < 16, r * rows, (r - 16) * rows + rows - 1)
    faces = jnp.where(c == want, 1.0, 0.0).astype(BF16)
    for g in range(planes // 16):
        block = state[g * 16 : g * 16 + 16].reshape(16 * rows, cols)
        got = jnp.dot(faces, block, preferred_element_type=F32).astype(BF16)
        top[g * 16 : g * 16 + 16, :] = got[0:16]
        bottom[g * 16 : g * 16 + 16, :] = got[16:32]
    er = lax.broadcasted_iota(jnp.int32, (SUB, LANES), 0)
    ec = lax.broadcasted_iota(jnp.int32, (SUB, LANES), 1)
    nt = (((1,), (1,)), ((), ()))
    pick_first = jnp.where(ec == 0, 1.0, 0.0).astype(BF16)
    pick_last = jnp.where(ec == LANES - 1, 1.0, 0.0).astype(BF16)
    left = state[:, :, 0:LANES].reshape(planes * rows, LANES)
    right = state[:, :, cols - LANES : cols].reshape(planes * rows, LANES)
    first[0] = lax.dot_general(pick_first, left, nt, preferred_element_type=F32)[0:1]
    last[0] = lax.dot_general(pick_last, right, nt, preferred_element_type=F32)[0:1]


def outgoing(modes, nodes, state):
    width, owned = modes.shape
    listed = nodes.shape[1]
    n, rows, cols = state.shape
    steps = 4
    planes = n // steps
    whole = lambda g: (0, 0)
    return pl.pallas_call(
        outgoing_kernel,
        grid=(steps,),
        in_specs=[
            pl.BlockSpec((width, owned), whole),
            pl.BlockSpec((1, listed), whole),
            pl.BlockSpec((planes, rows, cols), lambda g: (g, 0, 0)),
        ],
        out_specs=[
            pl.BlockSpec((listed, 2 * width), whole),
            pl.BlockSpec((planes, cols), lambda g: (g, 0)),
            pl.BlockSpec((planes, cols), lambda g: (g, 0)),
            pl.BlockSpec((1, 1, planes * rows), lambda g: (g, 0, 0)),
            pl.BlockSpec((1, 1, planes * rows), lambda g: (g, 0, 0)),
        ],
        out_shape=[
            jax.ShapeDtypeStruct((listed, 2 * width), BF16),
            jax.ShapeDtypeStruct((n, cols), BF16),
            jax.ShapeDtypeStruct((n, cols), BF16),
            jax.ShapeDtypeStruct((steps, 1, planes * rows), F32),
            jax.ShapeDtypeStruct((steps, 1, planes * rows), F32),
        ],
        scratch_shapes=[
            pltpu.VMEM((2 * width, owned), BF16),
            pltpu.VMEM((2 * width, min(listed, 256)), F32),
        ],
        compiler_params=pltpu.CompilerParams(vmem_limit_bytes=24 << 20),
    )(modes, nodes, state)


def inner_kernel(fields, jac, state, out, coef, centre, before, after):
    planes, rows, cols = state.shape
    blocks = cols // LANES
    high = rows // SUB

    @pl.when(pl.program_id(0) == 0)
    def _():
        for d, source in enumerate((0, 3, 4)):
            for m in range(VARS * VARS):
                for b in range(blocks):
                    for h in range(high):
                        coef[b * high + h, d * VARS * VARS + m] = jac[
                            source * VARS * VARS + m, h * SUB : h * SUB + SUB, b * LANES : b * LANES + LANES
                        ]

    flat = state[...].reshape(planes * rows, cols)
    shape = (planes, high, SUB, LANES)
    prior = jnp.dot(flat, diagonal(cols, cols, 1), preferred_element_type=F32)
    later = jnp.dot(flat, diagonal(cols, cols, -1), preferred_element_type=F32)
    here = state[...].astype(F32).reshape(planes * rows, cols)
    for b in range(blocks):
        at = slice(b * LANES, b * LANES + LANES)
        centre[b] = here[:, at].reshape(shape)
        before[b] = prior[:, at].reshape(shape)
        after[b] = later[:, at].reshape(shape)
    groups = planes // (fields * VARS)

    for b in range(blocks):
        kinds = [(0, centre)]
        if b > 0:
            kinds.append((1, before))
        if b < blocks - 1:
            kinds.append((2, after))

        def body(t, _, b=b, kinds=kinds):
            g = t // high
            h = t % high
            at = pl.ds(pl.multiple_of(h * SUB, SUB), SUB)
            acc = [[None] * VARS for _ in range(fields)]
            for d, source in kinds:
                for u in range(VARS):
                    q = [source[b, g * fields * VARS + f * VARS + u, h] for f in range(fields)]
                    for v in range(VARS):
                        j = coef[b * high + h, d * VARS * VARS + v * VARS + u]
                        for f in range(fields):
                            term = j * q[f]
                            acc[f][v] = term if acc[f][v] is None else acc[f][v] + term
            for f in range(fields):
                for v in range(VARS):
                    out[g * fields * VARS + f * VARS + v, at, b * LANES : b * LANES + LANES] = acc[f][v]
            return 0

        lax.fori_loop(0, groups * high, body, 0)


def inner_flux(jac, state):
    n, rows, cols = state.shape
    blocks = cols // LANES
    high = rows // SUB
    fields = 8
    planes = fields * VARS
    hold = pltpu.VMEM((blocks, planes, high, SUB, LANES), F32)
    return pl.pallas_call(
        functools.partial(inner_kernel, fields),
        grid=(n // planes,),
        in_specs=[
            pl.BlockSpec(jac.shape, lambda g: (0, 0, 0), pipeline_mode=pl.Buffered(1)),
            pl.BlockSpec((planes, rows, cols), lambda g: (g, 0, 0)),
        ],
        out_specs=pl.BlockSpec((planes, rows, cols), lambda g: (g, 0, 0)),
        out_shape=jax.ShapeDtypeStruct((n, rows, cols), F32),
        scratch_shapes=[pltpu.VMEM((blocks * high, 3 * VARS * VARS, SUB, LANES), F32), hold, hold, hold],
        compiler_params=pltpu.CompilerParams(vmem_limit_bytes=40 << 20),
        cost_estimate=pl.CostEstimate(flops=40_000_000_000, bytes_accessed=60_000_000, transcendentals=0),
    )(jac, state)


def outer_kernel(
    edge, freq, table, index, weight, blend, gain, volume, lower, upper, before, after, state,
    above, below, left, right, partial, motion, residual,
    modes, wide, side, shares, keys, w_hi, w_lo, moved,
):
    n, rows, _ = state.shape
    high = rows // SUB
    slots, width2 = table.shape
    width = width2 // 2
    entries = index.shape[0]
    cases = width // COMP
    jb = pl.program_id(0)
    blocks = pl.num_programs(0)

    @pl.when(jb == 0)
    def _():
        step = min(slots, 512)
        for b in range(slots // step):
            modes[:, b * step : b * step + step] = table[b * step : b * step + step, :].astype(F32).T.astype(BF16)

    live = [index[k] >= 0 for k in range(entries)]
    raw = [jnp.where(live[k], weight[k], 0.0) for k in range(entries)]
    total = raw[0]
    for k in range(1, entries):
        total = total + raw[k]
    scale = blend[...] / total
    share = [r * scale for r in raw]
    key = [index[k] for k in range(entries)]
    for k in range(entries):
        for m in range(k + 1, entries):
            same = key[k] == key[m]
            share[k] = jnp.where(same, share[k] + share[m], share[k])
            key[m] = jnp.where(same, -1, key[m])
    for k in range(entries):
        shares[k] = share[k]
        keys[k] = key[k]

    seg = 32
    slot_rows = lax.broadcasted_iota(jnp.int32, (seg, LANES), 0)

    def pair(i, _):
        for part in range(2):
            row = i * 2 + part
            at = slice(part * LANES, part * LANES + LANES)
            e = [jnp.broadcast_to(keys[k, pl.ds(row, 1), :], (SUB, LANES)) for k in range(entries)]
            w = [jnp.broadcast_to(shares[k, pl.ds(row, 1), :], (SUB, LANES)) for k in range(entries)]

            def build(s, _):
                base = pl.multiple_of(s * seg, seg)
                got = []
                for piece in range(seg // SUB):
                    ids = slot_rows[piece * SUB : piece * SUB + SUB] + base
                    value = jnp.where(ids == e[0], w[0], 0.0)
                    for k in range(1, entries):
                        value = jnp.where(ids == e[k], w[k], value)
                    got.append(value)
                hi, lo = halves(jnp.concatenate(got, axis=0))
                w_hi[pl.ds(base, seg), at] = hi
                w_lo[pl.ds(base, seg), at] = lo
                return 0

            lax.fori_loop(0, slots // seg, build, 0)
        both = jnp.dot(modes[...], w_hi[...], preferred_element_type=F32)
        rest = jnp.dot(modes[0:width, :], w_lo[...], preferred_element_type=F32)
        sums = both[0:width] + both[width:] + rest
        for part in range(2):
            at = slice(part * LANES, part * LANES + LANES)
            for c in range(width // SUB):
                moved[pl.ds(c * SUB * rows + i * 2 + part, SUB, stride=rows), :] = sums[c * SUB : c * SUB + SUB, at]
        return 0

    lax.fori_loop(0, rows // 2, pair, 0)
    for c in range(width):
        motion[c] = moved[c * rows : c * rows + rows, :]

    pitch = rows + 2 * SUB
    for p in range(n):
        wide[p * pitch + SUB : p * pitch + SUB + rows, :] = state[p].astype(F32)
    has_above = edge[0].astype(F32)
    has_below = edge[1].astype(F32)
    for g in range(n // 16):
        up = above[g * 16 : g * 16 + 16, :].astype(F32) * has_above
        down = below[g * 16 : g * 16 + 16, :].astype(F32) * has_below
        for half in range(2):
            start = (g * 16 + half * SUB) * pitch
            wide[pl.ds(start + SUB - 1, SUB, stride=pitch), :] = up[half * SUB : half * SUB + SUB]
            wide[pl.ds(start + SUB + rows, SUB, stride=pitch), :] = down[half * SUB : half * SUB + SUB]

    fields = 8
    lane = lax.broadcasted_iota(jnp.int32, (SUB, LANES), 1)

    def combine(extra):
        def body(t, _):
            g = t // high
            h = t % high
            at = pl.ds(pl.multiple_of(h * SUB, SUB), SUB)
            first = g * fields * VARS
            acc = [[partial[first + f * VARS + v, at, :] for v in range(VARS)] for f in range(fields)]
            for block, shift in ((lower, -1), (upper, 1)):
                for u in range(VARS):
                    q = [wide[pl.ds((first + f * VARS + u) * pitch + SUB + h * SUB + shift, SUB), :] for f in range(fields)]
                    for v in range(VARS):
                        j = block[v * VARS + u, at, :]
                        for f in range(fields):
                            acc[f][v] = acc[f][v] + j * q[f]
            if extra is not None:
                for u in range(VARS):
                    q = [side[first + f * VARS + u, at, :] for f in range(fields)]
                    for v in range(VARS):
                        j = extra[v * VARS + u, at, :]
                        for f in range(fields):
                            acc[f][v] = acc[f][v] + j * q[f]
            vol = volume[at, :]
            for c in range(fields // PARTS):
                case = g * (fields // PARTS) + c
                omega = freq[case]
                rate = vol * omega
                m = [moved[pl.ds((case * COMP + x) * rows + h * SUB, SUB), :] for x in range(COMP)]
                for v in range(VARS):
                    re = wide[pl.ds((first + c * 2 * VARS + v) * pitch + SUB + h * SUB, SUB), :]
                    im = wide[pl.ds((first + (c * 2 + 1) * VARS + v) * pitch + SUB + h * SUB, SUB), :]
                    pos = acc[2 * c][v] - rate * im
                    vel = gain[(VARS + v) * COMP, at, :] * m[0]
                    for x in range(COMP):
                        pos = pos + gain[v * COMP + x, at, :] * m[x]
                        if x > 0:
                            vel = vel + gain[(VARS + v) * COMP + x, at, :] * m[x]
                    residual[first + c * 2 * VARS + v, at, :] = pos
                    residual[first + (c * 2 + 1) * VARS + v, at, :] = acc[2 * c + 1][v] + rate * re + omega * vel
            return 0

        lax.fori_loop(0, n // (fields * VARS) * high, body, 0)

    def sideways(columns, flag, shift, edge_lane):
        steps, _, length = columns.shape
        group = LANES // rows
        for s in range(steps):
            for b in range(length // LANES):
                line = jnp.broadcast_to(columns[s, :, b * LANES : b * LANES + LANES] * flag, (SUB, LANES))
                stood = line.T
                for q in range(group):
                    p = (s * length + b * LANES) // rows + q
                    column = stood[q * rows : q * rows + rows, 0:1]
                    for h in range(high):
                        here = wide[p * pitch + SUB + h * SUB : p * pitch + SUB + h * SUB + SUB, :]
                        moved_over = pltpu.roll(here, shift, 1)
                        value = jnp.broadcast_to(column[h * SUB : h * SUB + SUB], (SUB, LANES))
                        side[p, h * SUB : h * SUB + SUB, :] = jnp.where(lane == edge_lane, value, moved_over)

    @pl.when(jb == 0)
    def _():
        sideways(left, edge[2].astype(F32), 1, 0)
        combine(before)

    @pl.when((jb > 0) & (jb < blocks - 1))
    def _():
        combine(None)

    @pl.when(jb == blocks - 1)
    def _():
        sideways(right, edge[3].astype(F32), LANES - 1, LANES - 1)
        combine(after)


def finish(edge, freq, table, index, weight, blend, gain, volume, jac, state, above, below, left, right, partial):
    n, rows, cols = state.shape
    slots, width2 = table.shape
    width = width2 // 2
    entries = index.shape[0]
    blocks = cols // LANES
    scalar = pl.BlockSpec(memory_space=pltpu.SMEM)
    cell3 = lambda lead: pl.BlockSpec((lead, rows, LANES), lambda b: (0, 0, b))
    cell2 = pl.BlockSpec((rows, LANES), lambda b: (0, b))
    jblock = lambda d: pl.BlockSpec((VARS * VARS, rows, LANES), lambda b: (d, 0, b))
    line = pl.BlockSpec((n, LANES), lambda b: (0, b))
    ends = pl.BlockSpec(left.shape, lambda b: (0, 0, 0))
    return pl.pallas_call(
        outer_kernel,
        grid=(blocks,),
        in_specs=[
            scalar, scalar,
            pl.BlockSpec(table.shape, lambda b: (0, 0)),
            cell3(entries), cell3(entries), cell2, cell3(gain.shape[0]), cell2,
            jblock(1), jblock(2), jblock(3), jblock(4),
            cell3(n), line, line, ends, ends, cell3(n),
        ],
        out_specs=[cell3(width), cell3(n)],
        out_shape=[
            jax.ShapeDtypeStruct((width, rows, cols), F32),
            jax.ShapeDtypeStruct((n, rows, cols), F32),
        ],
        scratch_shapes=[
            pltpu.VMEM((width2, slots), BF16),
            pltpu.VMEM((n * (rows + 2 * SUB), LANES), F32),
            pltpu.VMEM((n, rows, LANES), F32),
            pltpu.VMEM((entries, rows, LANES), F32),
            pltpu.VMEM((entries, rows, LANES), jnp.int32),
            pltpu.VMEM((slots, 2 * LANES), BF16),
            pltpu.VMEM((slots, 2 * LANES), BF16),
            pltpu.VMEM((width * rows, LANES), F32),
        ],
        compiler_params=pltpu.CompilerParams(vmem_limit_bytes=56 << 20),
    )(edge, freq, table, index, weight, blend, gain, volume, jac, jac, jac, jac, state, above, below, left, right, partial)


def ring(axis, step):
    peers = lax.axis_size(axis)
    return [(i, (i + step) % peers) for i in range(peers)]


def local(mode_shapes, send_nodes, interp_index, interp_weight, blend, motion_gain, frequency, volume, jacobian, state):
    axes = ("group", "dom")
    table, top, bottom, first, last = outgoing(mode_shapes, send_nodes, state)
    peers = lax.axis_size(axes)
    listed, width2 = table.shape
    arrived = lax.all_to_all(
        table.reshape(peers, listed // peers, width2), axes, split_axis=0, concat_axis=0, tiled=True
    ).reshape(listed, width2)
    above = lax.ppermute(bottom, "group", ring("group", 1))
    below = lax.ppermute(top, "group", ring("group", -1))
    left = lax.ppermute(last, "dom", ring("dom", 1))
    right = lax.ppermute(first, "dom", ring("dom", -1))
    gi, gn = lax.axis_index("group"), lax.axis_size("group")
    di, dn = lax.axis_index("dom"), lax.axis_size("dom")
    edge = jnp.stack([gi > 0, gi < gn - 1, di > 0, di < dn - 1]).astype(jnp.int32)
    partial = inner_flux(jacobian, state)
    return tuple(
        finish(
            edge, frequency, arrived, interp_index, interp_weight, blend, motion_gain, volume, jacobian, state,
            above, below, left, right, partial,
        )
    )


def solution(mesh):
    both = ("group", "dom")
    cells3 = P(None, "group", "dom")
    cells2 = P("group", "dom")
    placed = (P(None, both), P(both, None), cells3, cells3, cells2, cells3, P(), cells2, cells3, cells3)
    return jax.shard_map(local, mesh=mesh, in_specs=placed, out_specs=(cells3, cells3), check_vma=False)
```

```python
import functools
import jax
import jax.numpy as jnp
from jax import lax
from jax.experimental import pallas as pl
from jax.experimental.pallas import tpu as pltpu
from jax.sharding import PartitionSpec as P

COMP = 3
VARS = 5
PARTS = 2
LANES = 128
SUB = 8
FIELDS = 8
F32 = jnp.float32
BF16 = jnp.bfloat16


def halves(value):
    hi = value.astype(BF16)
    lo = (value - hi.astype(F32)).astype(BF16)
    return hi, lo


def diagonal(rows, cols, offset):
    r = lax.broadcasted_iota(jnp.int32, (rows, cols), 0)
    c = lax.broadcasted_iota(jnp.int32, (rows, cols), 1)
    return jnp.where(r + offset == c, 1.0, 0.0).astype(BF16)


def faces_kernel(state, top, bottom, first, last):
    planes, rows, cols = state.shape
    r = lax.broadcasted_iota(jnp.int32, (32, 16 * rows), 0)
    c = lax.broadcasted_iota(jnp.int32, (32, 16 * rows), 1)
    want = jnp.where(r < 16, r * rows, (r - 16) * rows + rows - 1)
    ends = jnp.where(c == want, 1.0, 0.0).astype(BF16)
    for g in range(planes // 16):
        block = state[g * 16 : g * 16 + 16].reshape(16 * rows, cols)
        got = jnp.dot(ends, block, preferred_element_type=F32).astype(BF16)
        top[g * 16 : g * 16 + 16, :] = got[0:16]
        bottom[g * 16 : g * 16 + 16, :] = got[16:32]
    ec = lax.broadcasted_iota(jnp.int32, (SUB, LANES), 1)
    nt = (((1,), (1,)), ((), ()))
    pick_first = jnp.where(ec == 0, 1.0, 0.0).astype(BF16)
    pick_last = jnp.where(ec == LANES - 1, 1.0, 0.0).astype(BF16)
    left = state[:, :, 0:LANES].reshape(planes * rows, LANES)
    right = state[:, :, cols - LANES : cols].reshape(planes * rows, LANES)
    got_first = lax.dot_general(pick_first, left, nt, preferred_element_type=F32)
    got_last = lax.dot_general(pick_last, right, nt, preferred_element_type=F32)
    parts, _, length = first.shape
    for q in range(parts):
        first[q] = got_first[0:1, q * length : (q + 1) * length]
        last[q] = got_last[0:1, q * length : (q + 1) * length]


def faces(state):
    n, rows, cols = state.shape
    steps = 4
    planes = n // steps
    chunk = planes // (FIELDS * VARS)
    length = FIELDS * VARS * rows
    face = pl.BlockSpec((planes, cols), lambda g: (g, 0))
    ends = pl.BlockSpec((chunk, 1, length), lambda g: (g, 0, 0))
    return pl.pallas_call(
        faces_kernel,
        grid=(steps,),
        in_specs=[pl.BlockSpec((planes, rows, cols), lambda g: (g, 0, 0))],
        out_specs=[face, face, ends, ends],
        out_shape=[
            jax.ShapeDtypeStruct((n, cols), BF16),
            jax.ShapeDtypeStruct((n, cols), BF16),
            jax.ShapeDtypeStruct((steps * chunk, 1, length), F32),
            jax.ShapeDtypeStruct((steps * chunk, 1, length), F32),
        ],
        compiler_params=pltpu.CompilerParams(vmem_limit_bytes=60 << 20),
    )(state)


def pick_kernel(modes, nodes, after, table, split, picked):
    width, owned = modes.shape
    listed = nodes.shape[1]
    hi, lo = halves(modes[...])
    split[0:width] = hi
    split[width:] = lo
    step = min(listed, 256)
    node_rows = lax.broadcasted_iota(jnp.int32, (owned, step), 0)

    def pick(b, _):
        at = pl.ds(pl.multiple_of(b * step, step), step)
        onehot = jnp.where(node_rows == nodes[:, at], 1.0, 0.0).astype(BF16)
        picked[...] = jnp.dot(split[...], onehot, preferred_element_type=F32)
        table[at, :] = picked[...].T.astype(BF16)
        return 0

    lax.fori_loop(0, listed // step, pick, 0)


def pick_nodes(modes, nodes, after):
    width, owned = modes.shape
    listed = nodes.shape[1]
    vmem = pl.BlockSpec(memory_space=pltpu.VMEM)
    return pl.pallas_call(
        pick_kernel,
        in_specs=[vmem, vmem, pl.BlockSpec(memory_space=pl.ANY)],
        out_specs=vmem,
        out_shape=jax.ShapeDtypeStruct((listed, 2 * width), BF16),
        scratch_shapes=[
            pltpu.VMEM((2 * width, owned), BF16),
            pltpu.VMEM((2 * width, min(listed, 256)), F32),
        ],
        compiler_params=pltpu.CompilerParams(vmem_limit_bytes=60 << 20),
    )(modes, nodes, after)


def flux_kernel(edge, freq, volume, jac, state, above, below, left, right, out, coef, wide, side, halo, arrive):
    planes, rows, cols = state.shape
    blocks = cols // LANES
    high = rows // SUB
    pitch = rows + 2 * SUB
    step = pl.program_id(0)

    def fetch(b):
        return pltpu.make_async_copy(jac.at[:, :, b * LANES : b * LANES + LANES], coef.at[b], arrive.at[b])

    @pl.when(step == 0)
    def _():
        for b in range(blocks):
            fetch(b).start()
        halo[0] = above[...].astype(F32) * edge[0].astype(F32)
        halo[1] = below[...].astype(F32) * edge[1].astype(F32)

    for p in range(planes):
        here = state[p].astype(F32)
        for b in range(blocks):
            wide[b, p * pitch + SUB : p * pitch + SUB + rows, :] = here[:, b * LANES : b * LANES + LANES]
    for g in range(planes // SUB):
        at = pl.ds(pl.multiple_of(step * planes, SUB) + g * SUB, SUB)
        for b in range(blocks):
            over = slice(b * LANES, b * LANES + LANES)
            wide[b, pl.ds(g * SUB * pitch + SUB - 1, SUB, stride=pitch), :] = halo[0, at, over]
            wide[b, pl.ds(g * SUB * pitch + SUB + rows, SUB, stride=pitch), :] = halo[1, at, over]
    for which, columns in enumerate((left, right)):
        flag = edge[2 + which].astype(F32)
        for g in range(planes * rows // LANES):
            line = jnp.broadcast_to(columns[0, :, g * LANES : g * LANES + LANES] * flag, (LANES, LANES))
            side[which, g * LANES : g * LANES + LANES, :] = line.T

    lane = lax.broadcasted_iota(jnp.int32, (SUB, LANES), 1)
    for b in range(blocks):

        @pl.when(step == 0)
        def _(b=b):
            fetch(b).wait()

        def body(h, _, b=b):
            start = pl.multiple_of(h * SUB, SUB)
            at = pl.ds(start, SUB)

            def rowof(block, p, shift):
                return wide[block, pl.ds(p * pitch + SUB + shift + start, SUB), :]

            vol = volume[at, b * LANES : b * LANES + LANES]
            rates = [vol * freq[step * (FIELDS // PARTS) + c] for c in range(FIELDS // PARTS)]
            acc = [[None] * VARS for _ in range(FIELDS)]
            for u in range(VARS):
                base = [rowof(b, f * VARS + u, 0) for f in range(FIELDS)]
                for c in range(FIELDS // PARTS):
                    re, im = 2 * c, 2 * c + 1
                    for f, term in ((re, -(rates[c] * base[im])), (im, rates[c] * base[re])):
                        acc[f][u] = term if acc[f][u] is None else acc[f][u] + term
                for d in range(5):
                    q = base
                    if d == 1:
                        q = [rowof(b, f * VARS + u, -1) for f in range(FIELDS)]
                    elif d == 2:
                        q = [rowof(b, f * VARS + u, 1) for f in range(FIELDS)]
                    elif d > 2:
                        turn, fill, source = (1, LANES - 1, b - 1) if d == 3 else (LANES - 1, 0, b + 1)
                        q = []
                        for f in range(FIELDS):
                            p = f * VARS + u
                            if 0 <= source < blocks:
                                other = rowof(source, p, 0)
                            else:
                                other = side[d - 3, pl.ds(p * rows + start, SUB), :]
                            q.append(pltpu.roll(jnp.where(lane == fill, other, base[f]), turn, 1))
                    for v in range(VARS):
                        j = coef[b, d * VARS * VARS + v * VARS + u, at, :]
                        for f in range(FIELDS):
                            term = j * q[f]
                            acc[f][v] = term if acc[f][v] is None else acc[f][v] + term
            for f in range(FIELDS):
                for v in range(VARS):
                    out[f * VARS + v, at, b * LANES : b * LANES + LANES] = acc[f][v]
            return 0

        lax.fori_loop(0, high, body, 0)


def flux(edge, freq, volume, jac, state, above, below, left, right):
    n, rows, cols = state.shape
    blocks = cols // LANES
    planes = FIELDS * VARS
    scalar = pl.BlockSpec(memory_space=pltpu.SMEM)
    whole = lambda g: (0, 0)
    ends = pl.BlockSpec((1, 1, planes * rows), lambda g: (g, 0, 0))
    return pl.pallas_call(
        flux_kernel,
        grid=(n // planes,),
        in_specs=[
            scalar, scalar,
            pl.BlockSpec((rows, cols), whole),
            pl.BlockSpec(memory_space=pl.ANY),
            pl.BlockSpec((planes, rows, cols), lambda g: (g, 0, 0)),
            pl.BlockSpec((n, cols), whole), pl.BlockSpec((n, cols), whole),
            ends, ends,
        ],
        out_specs=pl.BlockSpec((planes, rows, cols), lambda g: (g, 0, 0)),
        out_shape=jax.ShapeDtypeStruct((n, rows, cols), F32),
        scratch_shapes=[
            pltpu.VMEM((blocks, jac.shape[0], rows, LANES), F32),
            pltpu.VMEM((blocks, planes * (rows + 2 * SUB), LANES), F32),
            pltpu.VMEM((2, planes * rows, LANES), F32),
            pltpu.VMEM((2, n, cols), F32),
            pltpu.SemaphoreType.DMA((blocks,)),
        ],
        compiler_params=pltpu.CompilerParams(vmem_limit_bytes=60 << 20),
        cost_estimate=pl.CostEstimate(flops=40_000_000_000, bytes_accessed=60_000_000, transcendentals=0),
    )(edge, freq, volume, jac, state, above, below, left, right)


SEG = 32
RANKS = 2
SPARE = 2


def finish_kernel(
    freq, table, index, weight, blend, gain, partial, motion, residual,
    modes, lists_e, lists_w, spare_e, spare_w, moved, even,
):
    slots, width2 = table.shape
    width = width2 // 2
    entries = index.shape[0]
    cases = width // COMP
    owners = slots // SEG

    @pl.when((pl.program_id(0) == 0) & (pl.program_id(1) == 0))
    def _():
        step = min(slots, 512)
        for b in range(slots // step):
            turned = table[b * step : b * step + step, :].astype(F32).T.astype(BF16)
            modes[:, b * step : b * step + step] = turned
            modes[0:width, slots + b * step : slots + b * step + step] = turned[0:width]
            modes[width:, slots + b * step : slots + b * step + step] = jnp.zeros((width, step), BF16)

    raw = [jnp.where(index[k] >= 0, weight[k], 0.0) for k in range(entries)]
    total = raw[0]
    for k in range(1, entries):
        total = total + raw[k]
    scale = blend[...] / total
    share = [r * scale for r in raw]
    key = [index[k] for k in range(entries)]
    for k in range(entries):
        for m in range(k + 1, entries):
            same = key[k] == key[m]
            share[k] = jnp.where(same, share[k] + share[m], share[k])
            key[m] = jnp.where(same, -1, key[m])
    owner = [jnp.where(e < 0, -1 - k, e // SEG) for k, e in enumerate(key)]
    zero = jnp.zeros(owner[0].shape, jnp.int32)
    spare = []
    listed = []
    count = zero
    for k in range(entries):
        rank = zero
        for m in range(k):
            rank = rank + jnp.where(owner[m] == owner[k], 1, 0)
        over = (rank >= RANKS) & (key[k] >= 0)
        spare.append(jnp.where(over, count, -1))
        count = count + jnp.where(over, 1, 0)
        listed.append(jnp.where(over | (key[k] < 0), -1, owner[k] + rank * owners))
    for o in range(entries - RANKS):
        e = zero - 1
        w = jnp.zeros(zero.shape, F32)
        for k in range(entries):
            hit = spare[k] == o
            e = jnp.where(hit, key[k], e)
            w = jnp.where(hit, share[k], w)
        spare_e[o] = e
        spare_w[o] = w

    local = [e % SEG for e in key]

    def fill(i, _):
        e = zero - 1
        w = jnp.zeros(zero.shape, F32)
        for k in range(entries):
            hit = listed[k] == i
            e = jnp.where(hit, local[k], e)
            w = jnp.where(hit, share[k], w)
        lists_e[i] = e
        lists_w[i] = w
        return 0

    lax.fori_loop(0, owners * RANKS, fill, 0, unroll=4)

    slot_rows = lax.broadcasted_iota(jnp.int32, (SUB, LANES), 0)
    places = [slot_rows + q * SUB for q in range(SEG // SUB)]

    def spread(ref, i, row):
        return jnp.broadcast_to(ref[i, pl.ds(row, 1), :], (SUB, LANES))

    def put(into, s, part, pairs):
        got = []
        for ids in places:
            value = 0.0
            for e, w in pairs:
                value = jnp.where(ids == e, w, value)
            got.append(value)
        high, low = halves(jnp.concatenate(got, axis=0))
        at = pl.multiple_of(s * SEG, SEG)
        into[pl.ds(at, SEG), part * LANES : part * LANES + LANES] = high
        into[pl.ds(at + slots, SEG), part * LANES : part * LANES + LANES] = low

    def product(source):
        got = jnp.dot(modes[...], source[...], preferred_element_type=F32)
        return got[0:width] + got[width:]

    def place(sums, pair, add=False):
        for part in range(2):
            for c in range(width // SUB):
                at = pl.ds(c * SUB * SUB + pair * 2 + part, SUB, stride=SUB)
                value = sums[c * SUB : c * SUB + SUB, part * LANES : part * LANES + LANES]
                moved[at, :] = moved[at, :] + value if add else value

    chunk = min(slots, 256)

    def tile(pair, first, extra):
        highs, lows = [], []
        for q in range(chunk // SEG):
            s = first + q
            sides = []
            for part in range(2):
                row = pair * 2 + part
                pairs = [(spread(lists_e, s + r * owners, row), spread(lists_w, s + r * owners, row)) for r in range(RANKS)]
                pairs += [(e - s * SEG, w) for e, w in extra[part]]
                got = []
                for ids in places:
                    value = 0.0
                    for e, w in pairs:
                        value = jnp.where(ids == e, w, value)
                    got.append(value)
                sides.append(halves(jnp.concatenate(got, axis=0)))
            highs.append(jnp.concatenate([sides[0][0], sides[1][0]], axis=1))
            lows.append(jnp.concatenate([sides[0][1], sides[1][1]], axis=1))
        return jnp.concatenate(highs, axis=0), jnp.concatenate(lows, axis=0)

    def one_pair(pair):
        extra = [[(spread(spare_e, o, pair * 2 + part), spread(spare_w, o, pair * 2 + part)) for o in range(SPARE)] for part in range(2)]
        both = rest = None
        for c in range(slots // chunk):
            high, low = tile(pair, c * (chunk // SEG), extra)
            at = slice(c * chunk, c * chunk + chunk)
            x = jnp.dot(modes[:, at], high, preferred_element_type=F32)
            y = jnp.dot(modes[0:width, at], low, preferred_element_type=F32)
            both = x if both is None else both + x
            rest = y if rest is None else rest + y
        place(both[0:width] + both[width:] + rest, pair)

    def step_pair(pair, _):
        one_pair(pair)
        return 0

    lax.fori_loop(0, SUB // 2, step_pair, 0)

    most = jnp.max(count)

    @pl.when(most > SPARE)
    def _():
        def again(o, _):
            def one(pair, _):
                for part in range(2):
                    row = pair * 2 + part
                    e, w = spread(spare_e, o, row), spread(spare_w, o, row)

                    def rebuild(s, _):
                        put(even, s, part, [(e - s * SEG, w)])
                        return 0

                    lax.fori_loop(0, owners, rebuild, 0)
                place(product(even), pair, True)
                return 0

            lax.fori_loop(0, SUB // 2, one, 0)
            return 0

        lax.fori_loop(SPARE, most, again, 0)

    gains = [gain[i] for i in range(2 * VARS * COMP)]

    def force(c, _):
        omega = freq[c]
        m = [moved[pl.ds(pl.multiple_of((c * COMP + x) * SUB, SUB), SUB), :] for x in range(COMP)]
        for x in range(COMP):
            motion[c * COMP + x] = m[x]
        for v in range(VARS):
            pos = gains[v * COMP] * m[0]
            vel = gains[(VARS + v) * COMP] * m[0]
            for x in range(1, COMP):
                pos = pos + gains[v * COMP + x] * m[x]
                vel = vel + gains[(VARS + v) * COMP + x] * m[x]
            at = c * PARTS * VARS + v
            residual[at] = partial[at] + pos
            residual[at + VARS] = partial[at + VARS] + omega * vel
        return 0

    lax.fori_loop(0, cases, force, 0, unroll=2)


def finish(freq, table, index, weight, blend, gain, partial):
    n, rows, cols = partial.shape
    slots, width2 = table.shape
    width = width2 // 2
    entries = index.shape[0]
    owners = slots // SEG
    cells = lambda lead: pl.BlockSpec((lead, SUB, LANES), lambda b, h: (0, h, b))
    flat = pl.BlockSpec((SUB, LANES), lambda b, h: (h, b))
    return pl.pallas_call(
        finish_kernel,
        grid=(cols // LANES, rows // SUB),
        in_specs=[
            pl.BlockSpec(memory_space=pltpu.SMEM),
            pl.BlockSpec(table.shape, lambda b, h: (0, 0)),
            cells(entries), cells(entries), flat, cells(gain.shape[0]), cells(n),
        ],
        out_specs=[cells(width), cells(n)],
        out_shape=[
            jax.ShapeDtypeStruct((width, rows, cols), F32),
            jax.ShapeDtypeStruct((n, rows, cols), F32),
        ],
        scratch_shapes=[
            pltpu.VMEM((width2, 2 * slots), BF16),
            pltpu.VMEM((owners * RANKS, SUB, LANES), jnp.int32),
            pltpu.VMEM((owners * RANKS, SUB, LANES), F32),
            pltpu.VMEM((entries - RANKS, SUB, LANES), jnp.int32),
            pltpu.VMEM((entries - RANKS, SUB, LANES), F32),
            pltpu.VMEM((width * SUB, LANES), F32),
            pltpu.VMEM((2 * slots, 2 * LANES), BF16),
        ],
        compiler_params=pltpu.CompilerParams(vmem_limit_bytes=60 << 20),
    )(freq, table, index, weight, blend, gain, partial)


def ring(axis, step):
    peers = lax.axis_size(axis)
    return [(i, (i + step) % peers) for i in range(peers)]


def local(mode_shapes, send_nodes, interp_index, interp_weight, blend, motion_gain, frequency, volume, jacobian, state):
    axes = ("group", "dom")
    top, bottom, first, last = faces(state)
    table = pick_nodes(mode_shapes, send_nodes, first)
    peers = lax.axis_size(axes)
    listed, width2 = table.shape
    above = lax.ppermute(bottom, "group", ring("group", 1))
    below = lax.ppermute(top, "group", ring("group", -1))
    left = lax.ppermute(last, "dom", ring("dom", 1))
    right = lax.ppermute(first, "dom", ring("dom", -1))
    arrived = lax.all_to_all(
        table.reshape(peers, listed // peers, width2), axes, split_axis=0, concat_axis=0, tiled=True
    ).reshape(listed, width2)
    gi, gn = lax.axis_index("group"), lax.axis_size("group")
    di, dn = lax.axis_index("dom"), lax.axis_size("dom")
    edge = jnp.stack([gi > 0, gi < gn - 1, di > 0, di < dn - 1]).astype(jnp.int32)
    partial = flux(edge, frequency, volume, jacobian, state, above, below, left, right)
    return tuple(finish(frequency, arrived, interp_index, interp_weight, blend, motion_gain, partial))


def solution(mesh):
    both = ("group", "dom")
    cells3 = P(None, "group", "dom")
    cells2 = P("group", "dom")
    placed = (P(None, both), P(both, None), cells3, cells3, cells2, cells3, P(), cells2, cells3, cells3)
    return jax.shard_map(local, mesh=mesh, in_specs=placed, out_specs=(cells3, cells3), check_vma=False)
```

```python
import functools
import jax
import jax.numpy as jnp
from jax import lax
from jax.experimental import pallas as pl
from jax.experimental.pallas import tpu as pltpu
from jax.sharding import PartitionSpec as P

COMP = 3
VARS = 5
PARTS = 2
LANES = 128
SUB = 8
FIELDS = 8
ORDER = (0, 3, 1, 4, 2)
F32 = jnp.float32
BF16 = jnp.bfloat16


def halves(value):
    hi = value.astype(BF16)
    lo = (value - hi.astype(F32)).astype(BF16)
    return hi, lo


def faces_kernel(source, top, bottom, first, last, state, plain, arrive):
    count, planes, rows, cols = state.shape
    copies = [
        pltpu.make_async_copy(source.at[s * planes : (s + 1) * planes], state.at[s], arrive.at[s]) for s in range(count)
    ]
    for copy in copies:
        copy.start()
    for s, copy in enumerate(copies):
        copy.wait()
        cut_faces(s, state.at[s], top, bottom, first, last, plain)


def cut_faces(step, state, top, bottom, first, last, plain):
    planes, rows, cols = state.shape
    group = 16
    for g in range(planes // group):
        for p in range(group):
            here = state[g * group + p].astype(F32)
            for b in range(cols // LANES):
                plain[b, p * rows : p * rows + rows, :] = here[:, b * LANES : b * LANES + LANES]
        at = slice(step * planes + g * group, step * planes + g * group + group)
        for b in range(cols // LANES):
            over = slice(b * LANES, b * LANES + LANES)
            for ref, row in ((top, 0), (bottom, rows - 1)):
                ref[at, over] = jnp.concatenate(
                    [plain[b, pl.ds(half * SUB * rows + row, SUB, stride=rows), :] for half in range(group // SUB)], axis=0
                ).astype(BF16)
    r = lax.broadcasted_iota(jnp.int32, (SUB, 2 * LANES), 0)
    c = lax.broadcasted_iota(jnp.int32, (SUB, 2 * LANES), 1)
    pick = jnp.where(c == r * (2 * LANES - 1), 1.0, 0.0).astype(BF16)
    nt = (((1,), (1,)), ((), ()))
    sides = jnp.concatenate([state[:, :, 0:LANES], state[:, :, cols - LANES : cols]], axis=2)
    got = lax.dot_general(pick, sides.reshape(planes * rows, 2 * LANES), nt, preferred_element_type=F32)
    _, _, length = first.shape
    parts = planes * rows // length
    for q in range(parts):
        first[step * parts + q] = got[0:1, q * length : (q + 1) * length]
        last[step * parts + q] = got[1:2, q * length : (q + 1) * length]


def faces(state):
    n, rows, cols = state.shape
    steps = 4
    planes = n // steps
    chunk = planes // (FIELDS * VARS)
    length = FIELDS * VARS * rows
    vmem = pl.BlockSpec(memory_space=pltpu.VMEM)
    return pl.pallas_call(
        faces_kernel,
        in_specs=[pl.BlockSpec(memory_space=pl.ANY)],
        out_specs=[vmem] * 4,
        out_shape=[
            jax.ShapeDtypeStruct((n, cols), BF16),
            jax.ShapeDtypeStruct((n, cols), BF16),
            jax.ShapeDtypeStruct((steps * chunk, 1, length), F32),
            jax.ShapeDtypeStruct((steps * chunk, 1, length), F32),
        ],
        scratch_shapes=[
            pltpu.VMEM((steps, planes, rows, cols), BF16),
            pltpu.VMEM((cols // LANES, 16 * rows, LANES), F32),
            pltpu.SemaphoreType.DMA((steps,)),
        ],
        compiler_params=pltpu.CompilerParams(vmem_limit_bytes=63 << 20),
    )(state)


def pick_kernel(modes, nodes, after, table, split):
    width, owned = modes.shape
    listed = nodes.shape[1]
    hi, lo = halves(modes[...])
    split[0:width] = hi
    split[width:] = lo
    step = min(listed, 256)
    deep = min(owned, 256)
    node_rows = lax.broadcasted_iota(jnp.int32, (deep, step), 0)

    def pick(b, _):
        at = pl.ds(pl.multiple_of(b * step, step), step)
        wanted = jnp.broadcast_to(nodes[:, at], (deep, step))
        total = None
        for k in range(owned // deep):
            onehot = jnp.where(node_rows == wanted - k * deep, 1.0, 0.0).astype(BF16)
            part = jnp.dot(split[:, k * deep : k * deep + deep], onehot, preferred_element_type=F32)
            total = part if total is None else total + part
        table[at, :] = total.T.astype(BF16)
        return 0

    lax.fori_loop(0, listed // step, pick, 0)


def pick_nodes(modes, nodes, after):
    width, owned = modes.shape
    listed = nodes.shape[1]
    vmem = pl.BlockSpec(memory_space=pltpu.VMEM)
    return pl.pallas_call(
        pick_kernel,
        in_specs=[vmem, vmem, pl.BlockSpec(memory_space=pl.ANY)],
        out_specs=vmem,
        out_shape=jax.ShapeDtypeStruct((listed, 2 * width), BF16),
        scratch_shapes=[pltpu.VMEM((2 * width, owned), BF16)],
        compiler_params=pltpu.CompilerParams(vmem_limit_bytes=63 << 20),
    )(modes, nodes, after)


def flux_kernel(flags, freq, volume, jac, state, above, below, left, right, out, coef, wide, side, halo, arrive):
    planes, rows, cols = state.shape
    blocks = cols // LANES
    high = rows // SUB
    pitch = rows + 2 * SUB
    step = pl.program_id(0)
    place = [lax.axis_index(axis) for axis in ("group", "dom")]
    edge = [part for i, n in zip(place, flags) for part in (i > 0, i < n - 1)]

    def fetch(b):
        return pltpu.make_async_copy(jac.at[:, :, b * LANES : b * LANES + LANES], coef.at[b], arrive.at[b])

    @pl.when(step == 0)
    def _():
        for b in range(blocks):
            fetch(b).start()
        halo[0] = above[...].astype(F32) * jnp.where(edge[0], 1.0, 0.0)
        halo[1] = below[...].astype(F32) * jnp.where(edge[1], 1.0, 0.0)

    for p in range(planes):
        here = state[p].astype(F32)
        for b in range(blocks):
            wide[b, p * pitch + SUB : p * pitch + SUB + rows, :] = here[:, b * LANES : b * LANES + LANES]
    for g in range(planes // SUB):
        at = pl.ds(pl.multiple_of(step * planes, SUB) + g * SUB, SUB)
        for b in range(blocks):
            over = slice(b * LANES, b * LANES + LANES)
            wide[b, pl.ds(g * SUB * pitch + SUB - 1, SUB, stride=pitch), :] = halo[0, at, over]
            wide[b, pl.ds(g * SUB * pitch + SUB + rows, SUB, stride=pitch), :] = halo[1, at, over]
    for which, columns in enumerate((left, right)):
        flag = jnp.where(edge[2 + which], 1.0, 0.0)
        for g in range(planes * rows // LANES):
            line = jnp.broadcast_to(columns[0, :, g * LANES : g * LANES + LANES] * flag, (LANES, LANES))
            side[which, g * LANES : g * LANES + LANES, :] = line.T

    lane = lax.broadcasted_iota(jnp.int32, (SUB, LANES), 1)
    for b in range(blocks):

        @pl.when(step == 0)
        def _(b=b):
            fetch(b).wait()

        def body(h, _, b=b):
            start = pl.multiple_of(h * SUB, SUB)
            at = pl.ds(start, SUB)

            def rowof(block, p, shift):
                return wide[block, pl.ds(p * pitch + SUB + shift + start, SUB), :]

            vol = volume[at, b * LANES : b * LANES + LANES]
            rates = [vol * freq[step * (FIELDS // PARTS) + c] for c in range(FIELDS // PARTS)]
            acc = [[None] * VARS for _ in range(FIELDS)]

            def operand(u, d):
                centre = [rowof(b, f * VARS + u, 0) for f in range(FIELDS)] if d != 1 and d != 2 else None
                if d == 0:
                    return centre
                if d == 1:
                    return [rowof(b, f * VARS + u, -1) for f in range(FIELDS)]
                if d == 2:
                    return [rowof(b, f * VARS + u, 1) for f in range(FIELDS)]
                turn, fill, source = (1, LANES - 1, b - 1) if d == 3 else (LANES - 1, 0, b + 1)
                q = []
                for f in range(FIELDS):
                    p = f * VARS + u
                    if 0 <= source < blocks:
                        other = rowof(source, p, 0)
                    else:
                        other = side[d - 3, pl.ds(p * rows + start, SUB), :]
                    q.append(pltpu.roll(jnp.where(lane == fill, other, centre[f]), turn, 1))
                return q

            stages = [(u, d) for u in range(VARS) for d in ORDER]
            ahead = operand(*stages[0])
            for n, (u, d) in enumerate(stages):
                q = ahead
                if n + 1 < len(stages):
                    ahead = operand(*stages[n + 1])
                if d == 0:
                    for c in range(FIELDS // PARTS):
                        re, im = 2 * c, 2 * c + 1
                        for f, term in ((re, -(rates[c] * q[im])), (im, rates[c] * q[re])):
                            acc[f][u] = term if acc[f][u] is None else acc[f][u] + term
                for v in range(VARS):
                    j = coef[b, d * VARS * VARS + v * VARS + u, at, :]
                    for f in range(FIELDS):
                        term = j * q[f]
                        acc[f][v] = term if acc[f][v] is None else acc[f][v] + term
            for f in range(FIELDS):
                for v in range(VARS):
                    out[f * VARS + v, at, b * LANES : b * LANES + LANES] = acc[f][v]
            return 0

        lax.fori_loop(0, high, body, 0)


def flux(freq, volume, jac, state, above, below, left, right):
    n, rows, cols = state.shape
    blocks = cols // LANES
    planes = FIELDS * VARS
    scalar = pl.BlockSpec(memory_space=pltpu.SMEM)
    whole = lambda g: (0, 0)
    ends = pl.BlockSpec((1, 1, planes * rows), lambda g: (g, 0, 0))
    return pl.pallas_call(
        functools.partial(flux_kernel, [lax.axis_size(axis) for axis in ("group", "dom")]),
        grid=(n // planes,),
        in_specs=[
            scalar,
            pl.BlockSpec((rows, cols), whole),
            pl.BlockSpec(memory_space=pl.ANY),
            pl.BlockSpec((planes, rows, cols), lambda g: (g, 0, 0)),
            pl.BlockSpec((n, cols), whole), pl.BlockSpec((n, cols), whole),
            ends, ends,
        ],
        out_specs=pl.BlockSpec((planes, rows, cols), lambda g: (g, 0, 0)),
        out_shape=jax.ShapeDtypeStruct((n, rows, cols), F32),
        scratch_shapes=[
            pltpu.VMEM((blocks, jac.shape[0], rows, LANES), F32),
            pltpu.VMEM((blocks, planes * (rows + 2 * SUB), LANES), F32),
            pltpu.VMEM((2, planes * rows, LANES), F32),
            pltpu.VMEM((2, n, cols), F32),
            pltpu.SemaphoreType.DMA((blocks,)),
        ],
        compiler_params=pltpu.CompilerParams(vmem_limit_bytes=63 << 20),
        cost_estimate=pl.CostEstimate(flops=40_000_000_000, bytes_accessed=60_000_000, transcendentals=0),
    )(freq, volume, jac, state, above, below, left, right)


SHIFT = 5
SEG = 1 << SHIFT
RANKS = 2
SPARE = 2


def lists_kernel(index, weight, blend, lists_e, lists_w, spare_e, spare_w, counts):
    entries = index.shape[0]
    owners = lists_e.shape[0] // RANKS

    raw = [jnp.where(index[k] >= 0, weight[k], 0.0) for k in range(entries)]
    total = raw[0]
    for k in range(1, entries):
        total = total + raw[k]
    scale = blend[...] / total
    share = [r * scale for r in raw]
    key = [index[k] for k in range(entries)]
    for k in range(entries):
        for m in range(k + 1, entries):
            same = key[k] == key[m]
            share[k] = jnp.where(same, share[k] + share[m], share[k])
            key[m] = jnp.where(same, -1, key[m])
    owner = [jnp.where(e < 0, -1 - k, e >> SHIFT) for k, e in enumerate(key)]
    zero = jnp.zeros(owner[0].shape, jnp.int32)
    spare = []
    listed = []
    count = zero
    for k in range(entries):
        rank = zero
        for m in range(k):
            rank = rank + jnp.where(owner[m] == owner[k], 1, 0)
        over = (rank >= RANKS) & (key[k] >= 0)
        spare.append(jnp.where(over, count, -1))
        count = count + jnp.where(over, 1, 0)
        listed.append(jnp.where(over | (key[k] < 0), -1, owner[k] + rank * owners))
    for o in range(entries - RANKS):
        e = zero - 1
        w = jnp.zeros(zero.shape, F32)
        for k in range(entries):
            hit = spare[k] == o
            e = jnp.where(hit, key[k], e)
            w = jnp.where(hit, share[k], w)
        spare_e[o] = e
        spare_w[o] = w

    local = [e & (SEG - 1) for e in key]

    def fill(i, _):
        e = zero - 1
        w = jnp.zeros(zero.shape, F32)
        for k in range(entries):
            hit = listed[k] == i
            e = jnp.where(hit, local[k], e)
            w = jnp.where(hit, share[k], w)
        lists_e[i] = e
        lists_w[i] = w
        return 0

    lax.fori_loop(0, owners * RANKS, fill, 0, unroll=4)
    counts[...] = count


def owner_lists(index, weight, blend, slots):
    entries, rows, cols = index.shape
    owners = slots // SEG
    cells = lambda lead: pl.BlockSpec((lead, rows, LANES), lambda b: (0, 0, b))
    flat = pl.BlockSpec((rows, LANES), lambda b: (0, b))
    made = [
        (owners * RANKS, jnp.int32), (owners * RANKS, F32), (entries - RANKS, jnp.int32), (entries - RANKS, F32),
    ]
    return pl.pallas_call(
        lists_kernel,
        grid=(cols // LANES,),
        in_specs=[cells(entries), cells(entries), flat],
        out_specs=[cells(lead) for lead, _ in made] + [flat],
        out_shape=[jax.ShapeDtypeStruct((lead, rows, cols), kind) for lead, kind in made]
        + [jax.ShapeDtypeStruct((rows, cols), jnp.int32)],
        compiler_params=pltpu.CompilerParams(vmem_limit_bytes=63 << 20),
        cost_estimate=pl.CostEstimate(flops=4_000_000_000, bytes_accessed=6_000_000, transcendentals=0),
    )(index, weight, blend)


def finish_kernel(
    freq, table, lists_e, lists_w, spare_e, spare_w, counts, gain, partial, motion, residual, modes, moved, even,
):
    slots, width2 = table.shape
    width = width2 // 2
    cases = width // COMP
    owners = slots // SEG

    @pl.when((pl.program_id(0) == 0) & (pl.program_id(1) == 0))
    def _():
        step = min(slots, 512)
        for b in range(slots // step):
            turned = table[b * step : b * step + step, :].astype(F32).T.astype(BF16)
            modes[:, b * step : b * step + step] = turned
            modes[0:width, slots + b * step : slots + b * step + step] = turned[0:width]
            modes[width:, slots + b * step : slots + b * step + step] = jnp.zeros((width, step), BF16)

    slot_rows = lax.broadcasted_iota(jnp.int32, (SUB, LANES), 0)
    places = [slot_rows + q * SUB for q in range(SEG // SUB)]

    def spread(ref, i, row):
        return jnp.broadcast_to(ref[i, pl.ds(row, 1), :], (SUB, LANES))

    def put(into, s, part, pairs):
        got = []
        for ids in places:
            value = 0.0
            for e, w in pairs:
                value = jnp.where(ids == e, w, value)
            got.append(value)
        high, low = halves(jnp.concatenate(got, axis=0))
        at = pl.multiple_of(s * SEG, SEG)
        into[pl.ds(at, SEG), part * LANES : part * LANES + LANES] = high
        into[pl.ds(at + slots, SEG), part * LANES : part * LANES + LANES] = low

    def product(source):
        got = jnp.dot(modes[...], source[...], preferred_element_type=F32)
        return got[0:width] + got[width:]

    def place(sums, pair, add=False):
        for part in range(2):
            for c in range(width // SUB):
                at = pl.ds(c * SUB * SUB + pair * 2 + part, SUB, stride=SUB)
                value = sums[c * SUB : c * SUB + SUB, part * LANES : part * LANES + LANES]
                moved[at, :] = moved[at, :] + value if add else value

    chunk = min(slots, 256)

    def tile(pair, first, extra):
        highs, lows = [], []
        for q in range(chunk // SEG):
            s = first + q
            sides = []
            for part in range(2):
                row = pair * 2 + part
                pairs = [(spread(lists_e, s + r * owners, row), spread(lists_w, s + r * owners, row)) for r in range(RANKS)]
                pairs += [(e - s * SEG, w) for e, w in extra[part]]
                got = []
                for ids in places:
                    value = 0.0
                    for e, w in pairs:
                        value = jnp.where(ids == e, w, value)
                    got.append(value)
                sides.append(halves(jnp.concatenate(got, axis=0)))
            highs.append(jnp.concatenate([sides[0][0], sides[1][0]], axis=1))
            lows.append(jnp.concatenate([sides[0][1], sides[1][1]], axis=1))
        return jnp.concatenate(highs, axis=0), jnp.concatenate(lows, axis=0)

    def one_pair(pair):
        extra = [[(spread(spare_e, o, pair * 2 + part), spread(spare_w, o, pair * 2 + part)) for o in range(SPARE)] for part in range(2)]
        both = rest = None
        for c in range(slots // chunk):
            high, low = tile(pair, c * (chunk // SEG), extra)
            at = slice(c * chunk, c * chunk + chunk)
            x = jnp.dot(modes[:, at], high, preferred_element_type=F32)
            y = jnp.dot(modes[0:width, at], low, preferred_element_type=F32)
            both = x if both is None else both + x
            rest = y if rest is None else rest + y
        place(both[0:width] + both[width:] + rest, pair)

    def step_pair(pair, _):
        one_pair(pair)
        return 0

    if owners <= 32:
        for pair in range(SUB // 2):
            one_pair(pair)
    else:
        lax.fori_loop(0, SUB // 2, step_pair, 0)

    count = counts[...]
    most = jnp.max(count)

    @pl.when(most > SPARE)
    def _():
        for pair in range(SUB // 2):

            def again(o, _, pair=pair):
                for part in range(2):
                    row = pair * 2 + part
                    e, w = spread(spare_e, o, row), spread(spare_w, o, row)

                    def rebuild(s, _):
                        put(even, s, part, [(e - s * SEG, w)])
                        return 0

                    lax.fori_loop(0, owners, rebuild, 0)
                place(product(even), pair, True)
                return 0

            lax.fori_loop(SPARE, jnp.max(count[pair * 2 : pair * 2 + 2]), again, 0)

    gains = [gain[i] for i in range(2 * VARS * COMP)]

    def force(c, _):
        omega = freq[c]
        m = [moved[pl.ds(pl.multiple_of((c * COMP + x) * SUB, SUB), SUB), :] for x in range(COMP)]
        for x in range(COMP):
            motion[c * COMP + x] = m[x]
        for v in range(VARS):
            pos = gains[v * COMP] * m[0]
            vel = gains[(VARS + v) * COMP] * m[0]
            for x in range(1, COMP):
                pos = pos + gains[v * COMP + x] * m[x]
                vel = vel + gains[(VARS + v) * COMP + x] * m[x]
            at = c * PARTS * VARS + v
            residual[at] = partial[at] + pos
            residual[at + VARS] = partial[at + VARS] + omega * vel
        return 0

    lax.fori_loop(0, cases, force, 0, unroll=2)


def finish(freq, table, lists, gain, partial):
    n, rows, cols = partial.shape
    slots, width2 = table.shape
    width = width2 // 2
    cells = lambda lead: pl.BlockSpec((lead, SUB, LANES), lambda b, h: (0, h, b))
    flat = pl.BlockSpec((SUB, LANES), lambda b, h: (h, b))
    return pl.pallas_call(
        finish_kernel,
        grid=(cols // LANES, rows // SUB),
        in_specs=[
            pl.BlockSpec(memory_space=pltpu.SMEM),
            pl.BlockSpec(table.shape, lambda b, h: (0, 0)),
            *[cells(x.shape[0]) for x in lists[:4]], flat, cells(gain.shape[0]), cells(n),
        ],
        out_specs=[cells(width), cells(n)],
        out_shape=[
            jax.ShapeDtypeStruct((width, rows, cols), F32),
            jax.ShapeDtypeStruct((n, rows, cols), F32),
        ],
        scratch_shapes=[
            pltpu.VMEM((width2, 2 * slots), BF16),
            pltpu.VMEM((width * SUB, LANES), F32),
            pltpu.VMEM((2 * slots, 2 * LANES), BF16),
        ],
        compiler_params=pltpu.CompilerParams(vmem_limit_bytes=63 << 20),
    )(freq, table, *lists, gain, partial)


def ring(axis, step):
    peers = lax.axis_size(axis)
    return [(i, (i + step) % peers) for i in range(peers)]


def local(mode_shapes, send_nodes, interp_index, interp_weight, blend, motion_gain, frequency, volume, jacobian, state):
    axes = ("group", "dom")
    top, bottom, first, last = faces(state)
    above = lax.ppermute(bottom, "group", ring("group", 1))
    below = lax.ppermute(top, "group", ring("group", -1))
    table = pick_nodes(mode_shapes, send_nodes, first)
    peers = lax.axis_size(axes)
    listed, width2 = table.shape
    table, first, last = lax.optimization_barrier((table, first, last))
    left = lax.ppermute(last, "dom", ring("dom", 1))
    right = lax.ppermute(first, "dom", ring("dom", -1))
    lists = owner_lists(interp_index, interp_weight, blend, listed)
    table, *lists = lax.optimization_barrier((table, *lists))
    arrived = lax.all_to_all(
        table.reshape(peers, listed // peers, width2), axes, split_axis=0, concat_axis=0, tiled=True
    ).reshape(listed, width2)
    partial = flux(frequency, volume, jacobian, state, above, below, left, right)
    return tuple(finish(frequency, arrived, lists, motion_gain, partial))


def solution(mesh):
    both = ("group", "dom")
    cells3 = P(None, "group", "dom")
    cells2 = P("group", "dom")
    placed = (P(None, both), P(both, None), cells3, cells3, cells2, cells3, P(), cells2, cells3, cells3)
    return jax.shard_map(local, mesh=mesh, in_specs=placed, out_specs=(cells3, cells3), check_vma=False)
```

```python
import functools
import jax
import jax.numpy as jnp
from jax import lax
from jax.experimental import pallas as pl
from jax.experimental.pallas import tpu as pltpu
from jax.sharding import PartitionSpec as P

COMP = 3
VARS = 5
PARTS = 2
LANES = 128
SUB = 8
FIELDS = 8
ORDER = (0, 3, 1, 4, 2)
F32 = jnp.float32
BF16 = jnp.bfloat16


def halves(value):
    hi = value.astype(BF16)
    lo = (value - hi.astype(F32)).astype(BF16)
    return hi, lo


def faces_kernel(source, top, bottom, first, last, state, plain, arrive):
    count, planes, rows, cols = state.shape
    copies = [
        pltpu.make_async_copy(source.at[s * planes : (s + 1) * planes], state.at[s], arrive.at[s]) for s in range(count)
    ]
    for copy in copies:
        copy.start()
    for s, copy in enumerate(copies):
        copy.wait()
        cut_faces(s, state.at[s], top, bottom, first, last, plain)


def cut_faces(step, state, top, bottom, first, last, plain):
    planes, rows, cols = state.shape
    group = 16
    for g in range(planes // group):
        for p in range(group):
            here = state[g * group + p].astype(F32)
            for b in range(cols // LANES):
                plain[b, p * rows : p * rows + rows, :] = here[:, b * LANES : b * LANES + LANES]
        at = slice(step * planes + g * group, step * planes + g * group + group)
        for b in range(cols // LANES):
            over = slice(b * LANES, b * LANES + LANES)
            for ref, row in ((top, 0), (bottom, rows - 1)):
                ref[at, over] = jnp.concatenate(
                    [plain[b, pl.ds(half * SUB * rows + row, SUB, stride=rows), :] for half in range(group // SUB)], axis=0
                ).astype(BF16)
    r = lax.broadcasted_iota(jnp.int32, (SUB, 2 * LANES), 0)
    c = lax.broadcasted_iota(jnp.int32, (SUB, 2 * LANES), 1)
    pick = jnp.where(c == r * (2 * LANES - 1), 1.0, 0.0).astype(BF16)
    nt = (((1,), (1,)), ((), ()))
    sides = jnp.concatenate([state[:, :, 0:LANES], state[:, :, cols - LANES : cols]], axis=2)
    got = lax.dot_general(pick, sides.reshape(planes * rows, 2 * LANES), nt, preferred_element_type=F32)
    _, _, length = first.shape
    parts = planes * rows // length
    for q in range(parts):
        first[step * parts + q] = got[0:1, q * length : (q + 1) * length]
        last[step * parts + q] = got[1:2, q * length : (q + 1) * length]


def faces(state):
    n, rows, cols = state.shape
    steps = 4
    planes = n // steps
    chunk = planes // (FIELDS * VARS)
    length = FIELDS * VARS * rows
    vmem = pl.BlockSpec(memory_space=pltpu.VMEM)
    return pl.pallas_call(
        faces_kernel,
        in_specs=[pl.BlockSpec(memory_space=pl.ANY)],
        out_specs=[vmem] * 4,
        out_shape=[
            jax.ShapeDtypeStruct((n, cols), BF16),
            jax.ShapeDtypeStruct((n, cols), BF16),
            jax.ShapeDtypeStruct((steps * chunk, 1, length), F32),
            jax.ShapeDtypeStruct((steps * chunk, 1, length), F32),
        ],
        scratch_shapes=[
            pltpu.VMEM((steps, planes, rows, cols), BF16),
            pltpu.VMEM((cols // LANES, 16 * rows, LANES), F32),
            pltpu.SemaphoreType.DMA((steps,)),
        ],
        compiler_params=pltpu.CompilerParams(vmem_limit_bytes=(64 << 20) - (64 << 10)),
    )(state)


def pick_kernel(modes, nodes, after, table, split):
    width, owned = modes.shape
    listed = nodes.shape[1]
    hi, lo = halves(modes[...])
    split[0:width] = hi
    split[width:] = lo
    step = min(listed, 256)
    deep = min(owned, 256)
    node_rows = lax.broadcasted_iota(jnp.int32, (deep, step), 0)

    def pick(b, _):
        at = pl.ds(pl.multiple_of(b * step, step), step)
        wanted = jnp.broadcast_to(nodes[:, at], (deep, step))
        total = None
        for k in range(owned // deep):
            onehot = jnp.where(node_rows == wanted - k * deep, 1.0, 0.0).astype(BF16)
            part = jnp.dot(split[:, k * deep : k * deep + deep], onehot, preferred_element_type=F32)
            total = part if total is None else total + part
        table[at, :] = total.T.astype(BF16)
        return 0

    lax.fori_loop(0, listed // step, pick, 0, unroll=4)


def pick_nodes(modes, nodes, after):
    width, owned = modes.shape
    listed = nodes.shape[1]
    vmem = pl.BlockSpec(memory_space=pltpu.VMEM)
    return pl.pallas_call(
        pick_kernel,
        in_specs=[vmem, vmem, pl.BlockSpec(memory_space=pl.ANY)],
        out_specs=vmem,
        out_shape=jax.ShapeDtypeStruct((listed, 2 * width), BF16),
        scratch_shapes=[pltpu.VMEM((2 * width, owned), BF16)],
        compiler_params=pltpu.CompilerParams(vmem_limit_bytes=(64 << 20) - (64 << 10)),
    )(modes, nodes, after)


def flux_kernel(flags, freq, volume, jac, state, above, below, left, right, out, coef, wide, side, halo, arrive):
    planes, rows, cols = state.shape
    blocks = cols // LANES
    high = rows // SUB
    pitch = rows + 2 * SUB
    step = pl.program_id(0)
    place = [lax.axis_index(axis) for axis in ("group", "dom")]
    edge = [part for i, n in zip(place, flags) for part in (i > 0, i < n - 1)]

    def fetch(b):
        return pltpu.make_async_copy(jac.at[:, :, b * LANES : b * LANES + LANES], coef.at[b], arrive.at[b])

    @pl.when(step == 0)
    def _():
        for b in range(blocks):
            fetch(b).start()
        halo[0] = above[...].astype(F32) * jnp.where(edge[0], 1.0, 0.0)
        halo[1] = below[...].astype(F32) * jnp.where(edge[1], 1.0, 0.0)

    for p in range(planes):
        here = state[p].astype(F32)
        for b in range(blocks):
            wide[b, p * pitch + SUB : p * pitch + SUB + rows, :] = here[:, b * LANES : b * LANES + LANES]
    for g in range(planes // SUB):
        at = pl.ds(pl.multiple_of(step * planes, SUB) + g * SUB, SUB)
        for b in range(blocks):
            over = slice(b * LANES, b * LANES + LANES)
            wide[b, pl.ds(g * SUB * pitch + SUB - 1, SUB, stride=pitch), :] = halo[0, at, over]
            wide[b, pl.ds(g * SUB * pitch + SUB + rows, SUB, stride=pitch), :] = halo[1, at, over]
    for which, columns in enumerate((left, right)):
        flag = jnp.where(edge[2 + which], 1.0, 0.0)
        for g in range(planes * rows // LANES):
            line = jnp.broadcast_to(columns[0, :, g * LANES : g * LANES + LANES] * flag, (LANES, LANES))
            side[which, g * LANES : g * LANES + LANES, :] = line.T

    lane = lax.broadcasted_iota(jnp.int32, (SUB, LANES), 1)
    for b in range(blocks):

        @pl.when(step == 0)
        def _(b=b):
            fetch(b).wait()

        def body(h, _, b=b):
            start = pl.multiple_of(h * SUB, SUB)
            at = pl.ds(start, SUB)

            def rowof(block, p, shift):
                return wide[block, pl.ds(p * pitch + SUB + shift + start, SUB), :]

            vol = volume[at, b * LANES : b * LANES + LANES]
            rates = [vol * freq[step * (FIELDS // PARTS) + c] for c in range(FIELDS // PARTS)]
            acc = [[None] * VARS for _ in range(FIELDS)]

            def operand(u, d):
                centre = [rowof(b, f * VARS + u, 0) for f in range(FIELDS)] if d != 1 and d != 2 else None
                if d == 0:
                    return centre
                if d == 1:
                    return [rowof(b, f * VARS + u, -1) for f in range(FIELDS)]
                if d == 2:
                    return [rowof(b, f * VARS + u, 1) for f in range(FIELDS)]
                turn, fill, source = (1, LANES - 1, b - 1) if d == 3 else (LANES - 1, 0, b + 1)
                q = []
                for f in range(FIELDS):
                    p = f * VARS + u
                    if 0 <= source < blocks:
                        other = rowof(source, p, 0)
                    else:
                        other = side[d - 3, pl.ds(p * rows + start, SUB), :]
                    q.append(pltpu.roll(jnp.where(lane == fill, other, centre[f]), turn, 1))
                return q

            stages = [(u, d) for u in range(VARS) for d in ORDER]
            ahead = operand(*stages[0])
            for n, (u, d) in enumerate(stages):
                q = ahead
                if n + 1 < len(stages):
                    ahead = operand(*stages[n + 1])
                if d == 0:
                    for c in range(FIELDS // PARTS):
                        re, im = 2 * c, 2 * c + 1
                        for f, term in ((re, -(rates[c] * q[im])), (im, rates[c] * q[re])):
                            acc[f][u] = term if acc[f][u] is None else acc[f][u] + term
                for v in range(VARS):
                    j = coef[b, d * VARS * VARS + v * VARS + u, at, :]
                    for f in range(FIELDS):
                        term = j * q[f]
                        acc[f][v] = term if acc[f][v] is None else acc[f][v] + term
            for f in range(FIELDS):
                for v in range(VARS):
                    out[b, h, f * VARS + v] = acc[f][v]
            return 0

        lax.fori_loop(0, high, body, 0)


def flux(freq, volume, jac, state, above, below, left, right):
    n, rows, cols = state.shape
    blocks = cols // LANES
    planes = FIELDS * VARS
    scalar = pl.BlockSpec(memory_space=pltpu.SMEM)
    whole = lambda g: (0, 0)
    ends = pl.BlockSpec((1, 1, planes * rows), lambda g: (g, 0, 0))
    return pl.pallas_call(
        functools.partial(flux_kernel, [lax.axis_size(axis) for axis in ("group", "dom")]),
        grid=(n // planes,),
        in_specs=[
            scalar,
            pl.BlockSpec((rows, cols), whole),
            pl.BlockSpec(memory_space=pl.ANY),
            pl.BlockSpec((planes, rows, cols), lambda g: (g, 0, 0)),
            pl.BlockSpec((n, cols), whole), pl.BlockSpec((n, cols), whole),
            ends, ends,
        ],
        out_specs=pl.BlockSpec((blocks, rows // SUB, planes, SUB, LANES), lambda g: (0, 0, g, 0, 0)),
        out_shape=jax.ShapeDtypeStruct((blocks, rows // SUB, n, SUB, LANES), F32),
        scratch_shapes=[
            pltpu.VMEM((blocks, jac.shape[0], rows, LANES), F32),
            pltpu.VMEM((blocks, planes * (rows + 2 * SUB), LANES), F32),
            pltpu.VMEM((2, planes * rows, LANES), F32),
            pltpu.VMEM((2, n, cols), F32),
            pltpu.SemaphoreType.DMA((blocks,)),
        ],
        compiler_params=pltpu.CompilerParams(vmem_limit_bytes=(64 << 20) - (64 << 10)),
        cost_estimate=pl.CostEstimate(flops=40_000_000_000, bytes_accessed=60_000_000, transcendentals=0),
    )(freq, volume, jac, state, above, below, left, right)


SHIFT = 5
SEG = 1 << SHIFT
RANKS = 2
SPARE = 2


def lists_kernel(index, weight, blend, lists_e, lists_w, spare_e, spare_w, counts):
    entries = index.shape[0]
    owners = lists_e.shape[2] // RANKS

    def tile(ref, i, value):
        for h in range(ref.shape[1]):
            ref[0, h, i] = value[h * SUB : h * SUB + SUB]

    raw = [jnp.where(index[k] >= 0, weight[k], 0.0) for k in range(entries)]
    total = raw[0]
    for k in range(1, entries):
        total = total + raw[k]
    scale = blend[...] / total
    share = [r * scale for r in raw]
    key = [index[k] for k in range(entries)]
    for k in range(entries):
        for m in range(k + 1, entries):
            same = key[k] == key[m]
            share[k] = jnp.where(same, share[k] + share[m], share[k])
            key[m] = jnp.where(same, -1, key[m])
    owner = [jnp.where(e < 0, -1 - k, e >> SHIFT) for k, e in enumerate(key)]
    zero = jnp.zeros(owner[0].shape, jnp.int32)
    spare = []
    listed = []
    count = zero
    for k in range(entries):
        rank = zero
        for m in range(k):
            rank = rank + jnp.where(owner[m] == owner[k], 1, 0)
        over = (rank >= RANKS) & (key[k] >= 0)
        spare.append(jnp.where(over, count, -1))
        count = count + jnp.where(over, 1, 0)
        listed.append(jnp.where(over | (key[k] < 0), -1, owner[k] + rank * owners))
    for o in range(entries - RANKS):
        e = zero - 1
        w = jnp.zeros(zero.shape, F32)
        for k in range(entries):
            hit = spare[k] == o
            e = jnp.where(hit, key[k], e)
            w = jnp.where(hit, share[k], w)
        tile(spare_e, o, e)
        tile(spare_w, o, w)

    local = [e & (SEG - 1) for e in key]

    def fill(i, _):
        e = zero - 1
        w = jnp.zeros(zero.shape, F32)
        for k in range(entries):
            hit = listed[k] == i
            e = jnp.where(hit, local[k], e)
            w = jnp.where(hit, share[k], w)
        tile(lists_e, i, e)
        tile(lists_w, i, w)
        return 0

    lax.fori_loop(0, owners * RANKS, fill, 0, unroll=4)
    tile(counts, 0, count)


def owner_lists(index, weight, blend, slots):
    entries, rows, cols = index.shape
    owners = slots // SEG
    high = rows // SUB
    cells = lambda lead: pl.BlockSpec((lead, rows, LANES), lambda b: (0, 0, b))
    flat = pl.BlockSpec((rows, LANES), lambda b: (0, b))
    made = [
        (owners * RANKS, jnp.int32), (owners * RANKS, F32), (entries - RANKS, jnp.int32), (entries - RANKS, F32),
        (1, jnp.int32),
    ]
    return pl.pallas_call(
        lists_kernel,
        grid=(cols // LANES,),
        in_specs=[cells(entries), cells(entries), flat],
        out_specs=[pl.BlockSpec((1, high, lead, SUB, LANES), lambda b: (b, 0, 0, 0, 0)) for lead, _ in made],
        out_shape=[jax.ShapeDtypeStruct((cols // LANES, high, lead, SUB, LANES), kind) for lead, kind in made],
        compiler_params=pltpu.CompilerParams(vmem_limit_bytes=(64 << 20) - (64 << 10)),
        cost_estimate=pl.CostEstimate(flops=4_000_000_000, bytes_accessed=6_000_000, transcendentals=0),
    )(index, weight, blend)


def finish_kernel(
    freq, table, lists_e, lists_w, spare_e, spare_w, counts, gain, partial, motion, residual, modes, moved, even,
):
    slots, width2 = table.shape
    width = width2 // 2
    cases = width // COMP
    owners = slots // SEG

    @pl.when((pl.program_id(0) == 0) & (pl.program_id(1) == 0))
    def _():
        step = min(slots, 512)
        for b in range(slots // step):
            turned = table[b * step : b * step + step, :].astype(F32).T.astype(BF16)
            modes[:, b * step : b * step + step] = turned
            modes[0:width, slots + b * step : slots + b * step + step] = turned[0:width]
            modes[width:, slots + b * step : slots + b * step + step] = jnp.zeros((width, step), BF16)

    slot_rows = lax.broadcasted_iota(jnp.int32, (SUB, LANES), 0)
    places = [slot_rows + q * SUB for q in range(SEG // SUB)]

    def spread(ref, i, row):
        return jnp.broadcast_to(ref[i, pl.ds(row, 1), :], (SUB, LANES))

    def put(into, s, part, pairs):
        got = []
        for ids in places:
            value = 0.0
            for e, w in pairs:
                value = jnp.where(ids == e, w, value)
            got.append(value)
        high, low = halves(jnp.concatenate(got, axis=0))
        at = pl.multiple_of(s * SEG, SEG)
        into[pl.ds(at, SEG), part * LANES : part * LANES + LANES] = high
        into[pl.ds(at + slots, SEG), part * LANES : part * LANES + LANES] = low

    def product(source):
        got = jnp.dot(modes[...], source[...], preferred_element_type=F32)
        return got[0:width] + got[width:]

    def place(sums, pair, add=False):
        for part in range(2):
            for c in range(width // SUB):
                at = pl.ds(c * SUB * SUB + pair * 2 + part, SUB, stride=SUB)
                value = sums[c * SUB : c * SUB + SUB, part * LANES : part * LANES + LANES]
                moved[at, :] = moved[at, :] + value if add else value

    chunk = min(slots, 256)

    def tile(pair, first, extra):
        highs, lows = [], []
        for q in range(chunk // SEG):
            s = first + q
            sides = []
            for part in range(2):
                row = pair * 2 + part
                pairs = [(spread(lists_e, s + r * owners, row), spread(lists_w, s + r * owners, row)) for r in range(RANKS)]
                pairs += [(e - s * SEG, w) for e, w in extra[part]]
                got = []
                for ids in places:
                    value = 0.0
                    for e, w in pairs:
                        value = jnp.where(ids == e, w, value)
                    got.append(value)
                sides.append(halves(jnp.concatenate(got, axis=0)))
            highs.append(jnp.concatenate([sides[0][0], sides[1][0]], axis=1))
            lows.append(jnp.concatenate([sides[0][1], sides[1][1]], axis=1))
        return jnp.concatenate(highs, axis=0), jnp.concatenate(lows, axis=0)

    def one_pair(pair):
        extra = [[(spread(spare_e, o, pair * 2 + part), spread(spare_w, o, pair * 2 + part)) for o in range(SPARE)] for part in range(2)]
        both = rest = None
        for c in range(slots // chunk):
            high, low = tile(pair, c * (chunk // SEG), extra)
            at = slice(c * chunk, c * chunk + chunk)
            x = jnp.dot(modes[:, at], high, preferred_element_type=F32)
            y = jnp.dot(modes[0:width, at], low, preferred_element_type=F32)
            both = x if both is None else both + x
            rest = y if rest is None else rest + y
        place(both[0:width] + both[width:] + rest, pair)

    def step_pair(pair, _):
        one_pair(pair)
        return 0

    if owners <= 32:
        for pair in range(SUB // 2):
            one_pair(pair)
    else:
        lax.fori_loop(0, SUB // 2, step_pair, 0)

    count = counts[0]
    most = jnp.max(count)

    @pl.when(most > SPARE)
    def _():
        for pair in range(SUB // 2):

            def again(o, _, pair=pair):
                for part in range(2):
                    row = pair * 2 + part
                    e, w = spread(spare_e, o, row), spread(spare_w, o, row)

                    def rebuild(s, _):
                        put(even, s, part, [(e - s * SEG, w)])
                        return 0

                    lax.fori_loop(0, owners, rebuild, 0)
                place(product(even), pair, True)
                return 0

            lax.fori_loop(SPARE, jnp.max(count[pair * 2 : pair * 2 + 2]), again, 0)

    gains = [gain[i] for i in range(2 * VARS * COMP)]

    def force(c, _):
        omega = freq[c]
        m = [moved[pl.ds(pl.multiple_of((c * COMP + x) * SUB, SUB), SUB), :] for x in range(COMP)]
        for x in range(COMP):
            motion[c * COMP + x] = m[x]
        for v in range(VARS):
            pos = gains[v * COMP] * m[0]
            vel = gains[(VARS + v) * COMP] * m[0]
            for x in range(1, COMP):
                pos = pos + gains[v * COMP + x] * m[x]
                vel = vel + gains[(VARS + v) * COMP + x] * m[x]
            at = c * PARTS * VARS + v
            residual[at] = partial[at] + pos
            residual[at + VARS] = partial[at + VARS] + omega * vel
        return 0

    lax.fori_loop(0, cases, force, 0, unroll=4)


def finish(freq, table, lists, gain, partial):
    blocks, high, n, _, _ = partial.shape
    rows, cols = high * SUB, blocks * LANES
    slots, width2 = table.shape
    width = width2 // 2
    cells = lambda lead: pl.BlockSpec((lead, SUB, LANES), lambda b, h: (0, h, b))
    tiles = lambda lead: pl.BlockSpec((None, None, lead, SUB, LANES), lambda b, h: (b, h, 0, 0, 0))
    return pl.pallas_call(
        finish_kernel,
        grid=(cols // LANES, rows // SUB),
        in_specs=[
            pl.BlockSpec(memory_space=pltpu.SMEM),
            pl.BlockSpec(table.shape, lambda b, h: (0, 0)),
            *[tiles(x.shape[2]) for x in lists], cells(gain.shape[0]), tiles(n),
        ],
        out_specs=[cells(width), cells(n)],
        out_shape=[
            jax.ShapeDtypeStruct((width, rows, cols), F32),
            jax.ShapeDtypeStruct((n, rows, cols), F32),
        ],
        scratch_shapes=[
            pltpu.VMEM((width2, 2 * slots), BF16),
            pltpu.VMEM((width * SUB, LANES), F32),
            pltpu.VMEM((2 * slots, 2 * LANES), BF16),
        ],
        compiler_params=pltpu.CompilerParams(vmem_limit_bytes=(64 << 20) - (64 << 10)),
    )(freq, table, *lists, gain, partial)


def ring(axis, step):
    peers = lax.axis_size(axis)
    return [(i, (i + step) % peers) for i in range(peers)]


def local(mode_shapes, send_nodes, interp_index, interp_weight, blend, motion_gain, frequency, volume, jacobian, state):
    axes = ("group", "dom")
    top, bottom, first, last = faces(state)
    above = lax.ppermute(bottom, "group", ring("group", 1))
    below = lax.ppermute(top, "group", ring("group", -1))
    table = pick_nodes(mode_shapes, send_nodes, first)
    peers = lax.axis_size(axes)
    listed, width2 = table.shape
    table, first, last = lax.optimization_barrier((table, first, last))
    left = lax.ppermute(last, "dom", ring("dom", 1))
    right = lax.ppermute(first, "dom", ring("dom", -1))
    lists = owner_lists(interp_index, interp_weight, blend, listed)
    table, *lists = lax.optimization_barrier((table, *lists))
    arrived = lax.all_to_all(
        table.reshape(peers, listed // peers, width2), axes, split_axis=0, concat_axis=0, tiled=True
    ).reshape(listed, width2)
    partial = flux(frequency, volume, jacobian, state, above, below, left, right)
    return tuple(finish(frequency, arrived, lists, motion_gain, partial))


def solution(mesh):
    both = ("group", "dom")
    cells3 = P(None, "group", "dom")
    cells2 = P("group", "dom")
    placed = (P(None, both), P(both, None), cells3, cells3, cells2, cells3, P(), cells2, cells3, cells3)
    return jax.shard_map(local, mesh=mesh, in_specs=placed, out_specs=(cells3, cells3), check_vma=False)
```

```python
import functools
import jax
import jax.numpy as jnp
from jax import lax
from jax.experimental import pallas as pl
from jax.experimental.pallas import tpu as pltpu
from jax.sharding import PartitionSpec as P

COMP = 3
VARS = 5
PARTS = 2
LANES = 128
SUB = 8
FIELDS = 8
ORDER = (0, 1, 2, 3, 4)
F32 = jnp.float32
BF16 = jnp.bfloat16


def halves(value):
    hi = value.astype(BF16)
    lo = (value - hi.astype(F32)).astype(BF16)
    return hi, lo


def faces_kernel(source, top, bottom, first, last, state, plain, arrive):
    count, planes, rows, cols = state.shape
    copies = [
        pltpu.make_async_copy(source.at[s * planes : (s + 1) * planes], state.at[s], arrive.at[s]) for s in range(count)
    ]
    for copy in copies:
        copy.start()
    for s, copy in enumerate(copies):
        copy.wait()
        cut_faces(s, state.at[s], top, bottom, first, last, plain)


def cut_faces(step, state, top, bottom, first, last, plain):
    planes, rows, cols = state.shape
    group = 16
    for g in range(planes // group):
        for p in range(group):
            here = state[g * group + p].astype(F32)
            for b in range(cols // LANES):
                plain[b, p * rows : p * rows + rows, :] = here[:, b * LANES : b * LANES + LANES]
        at = slice(step * planes + g * group, step * planes + g * group + group)
        for b in range(cols // LANES):
            over = slice(b * LANES, b * LANES + LANES)
            for ref, row in ((top, 0), (bottom, rows - 1)):
                ref[at, over] = jnp.concatenate(
                    [plain[b, pl.ds(half * SUB * rows + row, SUB, stride=rows), :] for half in range(group // SUB)], axis=0
                ).astype(BF16)
    r = lax.broadcasted_iota(jnp.int32, (SUB, 2 * LANES), 0)
    c = lax.broadcasted_iota(jnp.int32, (SUB, 2 * LANES), 1)
    pick = jnp.where(c == r * (2 * LANES - 1), 1.0, 0.0).astype(BF16)
    nt = (((1,), (1,)), ((), ()))
    sides = jnp.concatenate([state[:, :, 0:LANES], state[:, :, cols - LANES : cols]], axis=2)
    got = lax.dot_general(pick, sides.reshape(planes * rows, 2 * LANES), nt, preferred_element_type=F32)
    _, _, length = first.shape
    parts = planes * rows // length
    for q in range(parts):
        first[step * parts + q] = got[0:1, q * length : (q + 1) * length]
        last[step * parts + q] = got[1:2, q * length : (q + 1) * length]


def faces(state):
    n, rows, cols = state.shape
    steps = 4
    planes = n // steps
    chunk = planes // (FIELDS * VARS)
    length = FIELDS * VARS * rows
    vmem = pl.BlockSpec(memory_space=pltpu.VMEM)
    return pl.pallas_call(
        faces_kernel,
        in_specs=[pl.BlockSpec(memory_space=pl.ANY)],
        out_specs=[vmem] * 4,
        out_shape=[
            jax.ShapeDtypeStruct((n, cols), BF16),
            jax.ShapeDtypeStruct((n, cols), BF16),
            jax.ShapeDtypeStruct((steps * chunk, 1, length), F32),
            jax.ShapeDtypeStruct((steps * chunk, 1, length), F32),
        ],
        scratch_shapes=[
            pltpu.VMEM((steps, planes, rows, cols), BF16),
            pltpu.VMEM((cols // LANES, 16 * rows, LANES), F32),
            pltpu.SemaphoreType.DMA((steps,)),
        ],
        compiler_params=pltpu.CompilerParams(vmem_limit_bytes=(64 << 20) - (64 << 10)),
    )(state)


def pick_kernel(modes, nodes, after, table, split):
    width, owned = modes.shape
    listed = nodes.shape[1]
    hi, lo = halves(modes[...])
    split[0:width] = hi
    split[width:] = lo
    step = min(listed, 256)
    deep = min(owned, 256)
    node_rows = lax.broadcasted_iota(jnp.int32, (deep, step), 0)

    def pick(b, _):
        at = pl.ds(pl.multiple_of(b * step, step), step)
        wanted = jnp.broadcast_to(nodes[:, at], (deep, step))
        total = None
        for k in range(owned // deep):
            onehot = jnp.where(node_rows == wanted - k * deep, 1.0, 0.0).astype(BF16)
            part = jnp.dot(split[:, k * deep : k * deep + deep], onehot, preferred_element_type=F32)
            total = part if total is None else total + part
        table[at, :] = total.T.astype(BF16)
        return 0

    lax.fori_loop(0, listed // step, pick, 0, unroll=4)


def pick_nodes(modes, nodes, after):
    width, owned = modes.shape
    listed = nodes.shape[1]
    vmem = pl.BlockSpec(memory_space=pltpu.VMEM)
    return pl.pallas_call(
        pick_kernel,
        in_specs=[vmem, vmem, pl.BlockSpec(memory_space=pl.ANY)],
        out_specs=vmem,
        out_shape=jax.ShapeDtypeStruct((listed, 2 * width), BF16),
        scratch_shapes=[pltpu.VMEM((2 * width, owned), BF16)],
        compiler_params=pltpu.CompilerParams(vmem_limit_bytes=(64 << 20) - (64 << 10)),
    )(modes, nodes, after)


def flux_kernel(flags, freq, volume, jac, state, above, below, left, right, out, coef, wide, side, halo, arrive):
    planes, rows, cols = state.shape
    blocks = cols // LANES
    high = rows // SUB
    pitch = rows + 2 * SUB
    step = pl.program_id(0)
    place = [lax.axis_index(axis) for axis in ("group", "dom")]
    edge = [part for i, n in zip(place, flags) for part in (i > 0, i < n - 1)]

    def fetch(b):
        return pltpu.make_async_copy(jac.at[:, :, b * LANES : b * LANES + LANES], coef.at[b], arrive.at[b])

    @pl.when(step == 0)
    def _():
        for b in range(blocks):
            fetch(b).start()
        halo[0] = above[...].astype(F32) * jnp.where(edge[0], 1.0, 0.0)
        halo[1] = below[...].astype(F32) * jnp.where(edge[1], 1.0, 0.0)

    for p in range(planes):
        here = state[p].astype(F32)
        for b in range(blocks):
            wide[b, p * pitch + SUB : p * pitch + SUB + rows, :] = here[:, b * LANES : b * LANES + LANES]
    for g in range(planes // SUB):
        at = pl.ds(pl.multiple_of(step * planes, SUB) + g * SUB, SUB)
        for b in range(blocks):
            over = slice(b * LANES, b * LANES + LANES)
            wide[b, pl.ds(g * SUB * pitch + SUB - 1, SUB, stride=pitch), :] = halo[0, at, over]
            wide[b, pl.ds(g * SUB * pitch + SUB + rows, SUB, stride=pitch), :] = halo[1, at, over]
    for which, columns in enumerate((left, right)):
        flag = jnp.where(edge[2 + which], 1.0, 0.0)
        for g in range(planes * rows // LANES):
            line = jnp.broadcast_to(columns[0, :, g * LANES : g * LANES + LANES] * flag, (LANES, LANES))
            side[which, g * LANES : g * LANES + LANES, :] = line.T

    lane = lax.broadcasted_iota(jnp.int32, (SUB, LANES), 1)
    for b in range(blocks):

        @pl.when(step == 0)
        def _(b=b):
            fetch(b).wait()

        def body(h, _, b=b):
            start = pl.multiple_of(h * SUB, SUB)
            at = pl.ds(start, SUB)

            def rowof(block, p, shift):
                return wide[block, pl.ds(p * pitch + SUB + shift + start, SUB), :]

            vol = volume[at, b * LANES : b * LANES + LANES]
            rates = [vol * freq[step * (FIELDS // PARTS) + c] for c in range(FIELDS // PARTS)]
            backs = [-rate for rate in rates]
            acc = [[None] * VARS for _ in range(FIELDS)]

            def operand(u, d):
                centre = [rowof(b, f * VARS + u, 0) for f in range(FIELDS)] if d != 1 and d != 2 else None
                if d == 0:
                    return centre
                if d == 1:
                    return [rowof(b, f * VARS + u, -1) for f in range(FIELDS)]
                if d == 2:
                    return [rowof(b, f * VARS + u, 1) for f in range(FIELDS)]
                turn, fill, source = (1, LANES - 1, b - 1) if d == 3 else (LANES - 1, 0, b + 1)
                q = []
                for f in range(FIELDS):
                    p = f * VARS + u
                    if 0 <= source < blocks:
                        other = rowof(source, p, 0)
                    else:
                        other = side[d - 3, pl.ds(p * rows + start, SUB), :]
                    q.append(pltpu.roll(jnp.where(lane == fill, other, centre[f]), turn, 1))
                return q

            stages = [(u, d) for u in range(VARS) for d in ORDER]
            ahead = operand(*stages[0])
            for n, (u, d) in enumerate(stages):
                q = ahead
                if n + 1 < len(stages):
                    ahead = operand(*stages[n + 1])
                if d == 0:
                    for c in range(FIELDS // PARTS):
                        re, im = 2 * c, 2 * c + 1
                        for f, term in ((re, backs[c] * q[im]), (im, rates[c] * q[re])):
                            acc[f][u] = term if acc[f][u] is None else acc[f][u] + term
                for v in range(VARS):
                    j = coef[b, d * VARS * VARS + v * VARS + u, at, :]
                    for f in range(FIELDS):
                        term = j * q[f]
                        acc[f][v] = term if acc[f][v] is None else acc[f][v] + term
            for f in range(FIELDS):
                for v in range(VARS):
                    out[b, h, f * VARS + v] = acc[f][v]
            return 0

        lax.fori_loop(0, high, body, 0)


def flux(freq, volume, jac, state, above, below, left, right):
    n, rows, cols = state.shape
    blocks = cols // LANES
    planes = FIELDS * VARS
    scalar = pl.BlockSpec(memory_space=pltpu.SMEM)
    whole = lambda g: (0, 0)
    ends = pl.BlockSpec((1, 1, planes * rows), lambda g: (g, 0, 0))
    return pl.pallas_call(
        functools.partial(flux_kernel, [lax.axis_size(axis) for axis in ("group", "dom")]),
        grid=(n // planes,),
        in_specs=[
            scalar,
            pl.BlockSpec((rows, cols), whole),
            pl.BlockSpec(memory_space=pl.ANY),
            pl.BlockSpec((planes, rows, cols), lambda g: (g, 0, 0)),
            pl.BlockSpec((n, cols), whole), pl.BlockSpec((n, cols), whole),
            ends, ends,
        ],
        out_specs=pl.BlockSpec((blocks, rows // SUB, planes, SUB, LANES), lambda g: (0, 0, g, 0, 0)),
        out_shape=jax.ShapeDtypeStruct((blocks, rows // SUB, n, SUB, LANES), F32),
        scratch_shapes=[
            pltpu.VMEM((blocks, jac.shape[0], rows, LANES), F32),
            pltpu.VMEM((blocks, planes * (rows + 2 * SUB), LANES), F32),
            pltpu.VMEM((2, planes * rows, LANES), F32),
            pltpu.VMEM((2, n, cols), F32),
            pltpu.SemaphoreType.DMA((blocks,)),
        ],
        compiler_params=pltpu.CompilerParams(vmem_limit_bytes=(64 << 20) - (64 << 10)),
        cost_estimate=pl.CostEstimate(flops=40_000_000_000, bytes_accessed=60_000_000, transcendentals=0),
    )(freq, volume, jac, state, above, below, left, right)


SHIFT = 5
SEG = 1 << SHIFT
RANKS = 2
SPARE = 2


def lists_kernel(index, weight, blend, lists_e, lists_w, spare_e, spare_w, counts):
    entries = index.shape[0]
    owners = lists_e.shape[2] // RANKS

    def tile(ref, i, value):
        for h in range(ref.shape[1]):
            ref[0, h, i] = value[h * SUB : h * SUB + SUB]

    raw = [jnp.where(index[k] >= 0, weight[k], 0.0) for k in range(entries)]
    total = raw[0]
    for k in range(1, entries):
        total = total + raw[k]
    scale = blend[...] / total
    share = [r * scale for r in raw]
    key = [index[k] for k in range(entries)]
    for k in range(entries):
        for m in range(k + 1, entries):
            same = key[k] == key[m]
            share[k] = jnp.where(same, share[k] + share[m], share[k])
            key[m] = jnp.where(same, -1, key[m])
    owner = [jnp.where(e < 0, -1 - k, e >> SHIFT) for k, e in enumerate(key)]
    zero = jnp.zeros(owner[0].shape, jnp.int32)
    spare = []
    listed = []
    count = zero
    for k in range(entries):
        rank = zero
        for m in range(k):
            rank = rank + jnp.where(owner[m] == owner[k], 1, 0)
        over = (rank >= RANKS) & (key[k] >= 0)
        spare.append(jnp.where(over, count, -1))
        count = count + jnp.where(over, 1, 0)
        listed.append(jnp.where(over | (key[k] < 0), -1, owner[k] + rank * owners))
    for o in range(entries - RANKS):
        e = zero - 1
        w = jnp.zeros(zero.shape, F32)
        for k in range(entries):
            hit = spare[k] == o
            e = jnp.where(hit, key[k], e)
            w = jnp.where(hit, share[k], w)
        tile(spare_e, o, e)
        tile(spare_w, o, w)

    local = [e & (SEG - 1) for e in key]

    def fill(i, _):
        e = zero - 1
        w = jnp.zeros(zero.shape, F32)
        for k in range(entries):
            hit = listed[k] == i
            e = jnp.where(hit, local[k], e)
            w = jnp.where(hit, share[k], w)
        tile(lists_e, i, e)
        tile(lists_w, i, w)
        return 0

    lax.fori_loop(0, owners * RANKS, fill, 0, unroll=4)
    tile(counts, 0, count)


def owner_lists(index, weight, blend, slots):
    entries, rows, cols = index.shape
    owners = slots // SEG
    high = rows // SUB
    cells = lambda lead: pl.BlockSpec((lead, rows, LANES), lambda b: (0, 0, b))
    flat = pl.BlockSpec((rows, LANES), lambda b: (0, b))
    made = [
        (owners * RANKS, jnp.int32), (owners * RANKS, F32), (entries - RANKS, jnp.int32), (entries - RANKS, F32),
        (1, jnp.int32),
    ]
    return pl.pallas_call(
        lists_kernel,
        grid=(cols // LANES,),
        in_specs=[cells(entries), cells(entries), flat],
        out_specs=[pl.BlockSpec((1, high, lead, SUB, LANES), lambda b: (b, 0, 0, 0, 0)) for lead, _ in made],
        out_shape=[jax.ShapeDtypeStruct((cols // LANES, high, lead, SUB, LANES), kind) for lead, kind in made],
        compiler_params=pltpu.CompilerParams(vmem_limit_bytes=(64 << 20) - (64 << 10)),
        cost_estimate=pl.CostEstimate(flops=4_000_000_000, bytes_accessed=6_000_000, transcendentals=0),
    )(index, weight, blend)


def finish_kernel(
    freq, table, lists_e, lists_w, spare_e, spare_w, counts, gain, partial, motion, residual, modes, moved, even,
):
    slots, width2 = table.shape
    width = width2 // 2
    cases = width // COMP
    owners = slots // SEG

    @pl.when((pl.program_id(0) == 0) & (pl.program_id(1) == 0))
    def _():
        step = min(slots, 512)
        for b in range(slots // step):
            turned = table[b * step : b * step + step, :].astype(F32).T.astype(BF16)
            modes[:, b * step : b * step + step] = turned
            modes[0:width, slots + b * step : slots + b * step + step] = turned[0:width]
            modes[width:, slots + b * step : slots + b * step + step] = jnp.zeros((width, step), BF16)

    slot_rows = lax.broadcasted_iota(jnp.int32, (SUB, LANES), 0)
    places = [slot_rows + q * SUB for q in range(SEG // SUB)]

    def spread(ref, i, row):
        return jnp.broadcast_to(ref[i, pl.ds(row, 1), :], (SUB, LANES))

    def put(into, s, part, pairs):
        got = []
        for ids in places:
            value = 0.0
            for e, w in pairs:
                value = jnp.where(ids == e, w, value)
            got.append(value)
        high, low = halves(jnp.concatenate(got, axis=0))
        at = pl.multiple_of(s * SEG, SEG)
        into[pl.ds(at, SEG), part * LANES : part * LANES + LANES] = high
        into[pl.ds(at + slots, SEG), part * LANES : part * LANES + LANES] = low

    def product(source):
        got = jnp.dot(modes[...], source[...], preferred_element_type=F32)
        return got[0:width] + got[width:]

    def place(sums, pair, add=False):
        for part in range(2):
            for c in range(width // SUB):
                at = pl.ds(c * SUB * SUB + pair * 2 + part, SUB, stride=SUB)
                value = sums[c * SUB : c * SUB + SUB, part * LANES : part * LANES + LANES]
                moved[at, :] = moved[at, :] + value if add else value

    chunk = min(slots, 256)

    def tile(pair, first, extra):
        highs, lows = [], []
        for q in range(chunk // SEG):
            s = first + q
            sides = []
            for part in range(2):
                row = pair * 2 + part
                pairs = [(spread(lists_e, s + r * owners, row), spread(lists_w, s + r * owners, row)) for r in range(RANKS)]
                pairs += [(e - s * SEG, w) for e, w in extra[part]]
                got = []
                for ids in places:
                    value = 0.0
                    for e, w in pairs:
                        value = jnp.where(ids == e, w, value)
                    got.append(value)
                sides.append(halves(jnp.concatenate(got, axis=0)))
            highs.append(jnp.concatenate([sides[0][0], sides[1][0]], axis=1))
            lows.append(jnp.concatenate([sides[0][1], sides[1][1]], axis=1))
        return jnp.concatenate(highs, axis=0), jnp.concatenate(lows, axis=0)

    def one_pair(pair):
        extra = [[(spread(spare_e, o, pair * 2 + part), spread(spare_w, o, pair * 2 + part)) for o in range(SPARE)] for part in range(2)]
        both = rest = None
        for c in range(slots // chunk):
            high, low = tile(pair, c * (chunk // SEG), extra)
            at = slice(c * chunk, c * chunk + chunk)
            x = jnp.dot(modes[:, at], high, preferred_element_type=F32)
            y = jnp.dot(modes[0:width, at], low, preferred_element_type=F32)
            both = x if both is None else both + x
            rest = y if rest is None else rest + y
        place(both[0:width] + both[width:] + rest, pair)

    def step_pair(pair, _):
        one_pair(pair)
        return 0

    if owners <= 32:
        for pair in range(SUB // 2):
            one_pair(pair)
    else:
        lax.fori_loop(0, SUB // 2, step_pair, 0)

    count = counts[0]
    most = jnp.max(count)

    @pl.when(most > SPARE)
    def _():
        for pair in range(SUB // 2):

            def again(o, _, pair=pair):
                for part in range(2):
                    row = pair * 2 + part
                    e, w = spread(spare_e, o, row), spread(spare_w, o, row)

                    def rebuild(s, _):
                        put(even, s, part, [(e - s * SEG, w)])
                        return 0

                    lax.fori_loop(0, owners, rebuild, 0)
                place(product(even), pair, True)
                return 0

            lax.fori_loop(SPARE, jnp.max(count[pair * 2 : pair * 2 + 2]), again, 0)

    gains = [gain[i] for i in range(2 * VARS * COMP)]

    def force(c, _):
        omega = freq[c]
        m = [moved[pl.ds(pl.multiple_of((c * COMP + x) * SUB, SUB), SUB), :] for x in range(COMP)]
        for x in range(COMP):
            motion[c * COMP + x] = m[x]
        for v in range(VARS):
            pos = gains[v * COMP] * m[0]
            vel = gains[(VARS + v) * COMP] * m[0]
            for x in range(1, COMP):
                pos = pos + gains[v * COMP + x] * m[x]
                vel = vel + gains[(VARS + v) * COMP + x] * m[x]
            at = c * PARTS * VARS + v
            residual[at] = partial[at] + pos
            residual[at + VARS] = partial[at + VARS] + omega * vel
        return 0

    lax.fori_loop(0, cases, force, 0, unroll=8)


def finish(freq, table, lists, gain, partial):
    blocks, high, n, _, _ = partial.shape
    rows, cols = high * SUB, blocks * LANES
    slots, width2 = table.shape
    width = width2 // 2
    cells = lambda lead: pl.BlockSpec((lead, SUB, LANES), lambda b, h: (0, h, b))
    tiles = lambda lead: pl.BlockSpec((None, None, lead, SUB, LANES), lambda b, h: (b, h, 0, 0, 0))
    return pl.pallas_call(
        finish_kernel,
        grid=(cols // LANES, rows // SUB),
        in_specs=[
            pl.BlockSpec(memory_space=pltpu.SMEM),
            pl.BlockSpec(table.shape, lambda b, h: (0, 0)),
            *[tiles(x.shape[2]) for x in lists], cells(gain.shape[0]), tiles(n),
        ],
        out_specs=[cells(width), cells(n)],
        out_shape=[
            jax.ShapeDtypeStruct((width, rows, cols), F32),
            jax.ShapeDtypeStruct((n, rows, cols), F32),
        ],
        scratch_shapes=[
            pltpu.VMEM((width2, 2 * slots), BF16),
            pltpu.VMEM((width * SUB, LANES), F32),
            pltpu.VMEM((2 * slots, 2 * LANES), BF16),
        ],
        compiler_params=pltpu.CompilerParams(vmem_limit_bytes=(64 << 20) - (64 << 10)),
    )(freq, table, *lists, gain, partial)


def ring(axis, step):
    peers = lax.axis_size(axis)
    return [(i, (i + step) % peers) for i in range(peers)]


def local(mode_shapes, send_nodes, interp_index, interp_weight, blend, motion_gain, frequency, volume, jacobian, state):
    axes = ("group", "dom")
    top, bottom, first, last = faces(state)
    above = lax.ppermute(bottom, "group", ring("group", 1))
    below = lax.ppermute(top, "group", ring("group", -1))
    table = pick_nodes(mode_shapes, send_nodes, first)
    peers = lax.axis_size(axes)
    listed, width2 = table.shape
    table, first, last = lax.optimization_barrier((table, first, last))
    left = lax.ppermute(last, "dom", ring("dom", 1))
    right = lax.ppermute(first, "dom", ring("dom", -1))
    lists = owner_lists(interp_index, interp_weight, blend, listed)
    table, *lists = lax.optimization_barrier((table, *lists))
    arrived = lax.all_to_all(
        table.reshape(peers, listed // peers, width2), axes, split_axis=0, concat_axis=0, tiled=True
    ).reshape(listed, width2)
    partial = flux(frequency, volume, jacobian, state, above, below, left, right)
    return tuple(finish(frequency, arrived, lists, motion_gain, partial))


def solution(mesh):
    both = ("group", "dom")
    cells3 = P(None, "group", "dom")
    cells2 = P("group", "dom")
    placed = (P(None, both), P(both, None), cells3, cells3, cells2, cells3, P(), cells2, cells3, cells3)
    return jax.shard_map(local, mesh=mesh, in_specs=placed, out_specs=(cells3, cells3), check_vma=False)
```
